32 devices in a mesh: lat: 8 (over z, x), lon: 4 (over y, core).
Axes of the slice: x: 2, y: 2, z: 4, core: 2. Of those that a mesh axis runs over, the one named last changes fastest.
Arguments:
- grid_feat: bfloat16 [32768, 474], P(('lat', 'lon')), may hold values from -6 to 6
- grid_send: int32 [32, 4, 256], P(('lat', 'lon')), may hold values from 0 to 1023
- g2m_sender: int32 [131072], P(('lat', 'lon')), may hold values from 0 to 2047, as said below
- g2m_receiver: int32 [131072], P(('lat', 'lon')), may hold values from 0 to 320, as said below
- g2m_geom: float32 [4, 131072], P(None, ('lat', 'lon')), may hold values from -1 to 1
- mesh_geom: float32 [3, 10240], P(None, ('lat', 'lon')), may hold values from -1 to 1
- mesh_adjacent_lists: int32 [32, 8, 112], P(('lat', 'lon')), may hold values from 0 to 319
- mesh_far: int32 [32, 32, 4], P(('lat', 'lon')), may hold values from 0 to 319
- mesh_sender: int32 [131072], P(('lat', 'lon')), may hold values from 0 to 1343, as said below
- mesh_receiver: int32 [131072], P(('lat', 'lon')), may hold values from 0 to 320, as said below
- mesh_edge_geom: float32 [4, 131072], P(None, ('lat', 'lon')), may hold values from -1 to 1
- embed_in: bfloat16 [474, 512], replicated, may hold values from -0.25 to 0.25
- mesh_in: float32 [3, 512], replicated, may hold values from -3.5 to 3.5
- geo_in: float32 [3, 4, 512], replicated, may hold values from -3 to 3
- pair_in: bfloat16 [3, 4, 512, 512], replicated, may hold values from -0.1875 to 0.1875
- square_out: bfloat16 [8, 512, 512], replicated, may hold values from -0.25 to 0.25
Outputs:
- mesh_out: bfloat16 [10240, 512], P(('lat', 'lon'))
The draws below stay inside these ranges and needn't reach their ends.
Inputs may be any that keep to these rules, and one draw needn't show every extreme that they name: grid_send[s, d, k] is a local grid row of device s, which it sends to the device that has s as its source for side offset o_d. `g2m_sender`: below 1024, a local grid row of the edge's device; else 1024 + d * 256 + k, a row of received_grid whose source exists. `g2m_receiver`: a local mesh row of the edge's device, or 320 for a padding edge; a device's live edges come first, and some device has all 4096 live. mesh_adjacent_lists[t, d, k] is a local mesh row of device t, which it sends to the device that has t as its source for neighbour offset n_d. mesh_far[t, q, k] is a local mesh row of device t, which it sends to device q. `mesh_sender`: below 320, a local mesh row of the edge's device; else a halo row of the edge's device, and a neighbour's row only where that neighbour exists. `mesh_receiver`: a local mesh row of the edge's device, or 320 for a padding edge; a device's live edges come first, and some device has all 4096 live.
All inputs are finite; a program needn't handle non-finite values.
Results may differ from the reference program's by a relative error of at most 0.015.
Values may be sent and summed in bfloat16 or wider, within the bound.
No kernel may reach another device: no remote copies, remote signals or barrier semaphores. Data moves between devices by JAX's collectives and lax.ppermute only.
A program may use at most 128 MiB of HBM per device.

```python
import jax
import jax.numpy as jnp
from jax import lax

D = 512
C_IN = 474
GRID_DEV = 1024
GSLOT = 256
MESH_PER_DEVICE = 320
NEAR_ROW_SLOTS = 112
FAR_ROW_SLOTS = 4
E_G2M = 4096
E_MESH = 4096
STEPS = 2
GRID = 32768
MESH = 10240
G2M = 131072
MESH_EDGE_SLOTS = 131072
SECTIONS = 3
SQUARES = 8
N_LAT = 8
N_LON = 4
DEVICES = 32


GRID_LAT_STEPS = (-1, 1, 0, 0)


MESH_LATITUDES = (-1, -1, -1, 0, 0, 1, 1, 1)


def live_mask(seed_key, device_row_total, per_device):
    shifts = jax.random.randint(jax.random.fold_in(seed_key, 11), (device_row_total,), 0, 3)
    tallies = jnp.right_shift(jnp.full((device_row_total,), per_device, jnp.int32), shifts.astype(jnp.int32))
    fullest_device = jax.random.randint(jax.random.fold_in(seed_key, 12), (), 0, device_row_total)
    tallies = jnp.where(jnp.arange(device_row_total, dtype=jnp.int32) == fullest_device, per_device, tallies)
    return jnp.arange(per_device, dtype=jnp.int32)[None, :] < tallies[:, None]


def slot_tallies(seed_key, device_row_total, directions, bound, full_direction, fullest_device):
    tallies = jax.random.randint(jax.random.fold_in(seed_key, 1), (device_row_total, directions), 1, bound + 1)
    marked = jnp.logical_and(jnp.arange(device_row_total, dtype=jnp.int32)[:, None] == fullest_device, jnp.arange(directions, dtype=jnp.int32)[None, :] == full_direction)
    return jnp.where(marked, bound, tallies).astype(jnp.int32)


def adjacent_slot(seed_key, owning_device_ids, directions, lat_table, tallies, bound):
    total = owning_device_ids.shape[0]
    direction = jax.random.randint(jax.random.fold_in(seed_key, 3), (total,), 0, directions)
    lat_step = jnp.array(lat_table, dtype=jnp.int32)[direction]
    source_lat = owning_device_ids // N_LON - lat_step
    within_bounds = jnp.logical_and(source_lat >= 0, source_lat < N_LAT)
    spread = jax.random.randint(jax.random.fold_in(seed_key, 4), (total,), 0, 1 << 20)
    position = spread % tallies[owning_device_ids, direction]
    return ((direction * bound + position).astype(jnp.int32), within_bounds)


def draw_g2m_sender(key, part):
    device_row_total = G2M // E_G2M
    slot_numbers = jnp.arange(G2M, dtype=jnp.int32)
    owning_device_ids = slot_numbers // E_G2M
    fullest_device = jax.random.randint(jax.random.fold_in(key, 401), (), 0, device_row_total)
    tallies = slot_tallies(jax.random.fold_in(key, 402), device_row_total, 4, GSLOT, 3, fullest_device)
    adjacent_index, within_bounds = adjacent_slot(jax.random.fold_in(key, 403), owning_device_ids, 4, GRID_LAT_STEPS, tallies, GSLOT)
    chooser = jax.random.randint(jax.random.fold_in(key, 404), (G2M,), 0, 4)
    own_rows = jax.random.randint(jax.random.fold_in(key, 405), (G2M,), 0, GRID_DEV)
    final_output = jnp.where(jnp.logical_or(chooser < 2, jnp.logical_not(within_bounds)), own_rows, GRID_DEV + adjacent_index)
    starting_slot = fullest_device * E_G2M
    final_output = jnp.where(slot_numbers == starting_slot, GRID_DEV + 4 * GSLOT - 1, final_output)
    final_output = jnp.where(slot_numbers == starting_slot + 1, 0, final_output)
    return final_output.astype(jnp.int32)


def draw_g2m_receiver(key, part):
    device_row_total = G2M // E_G2M
    live_slots = live_mask(jax.random.fold_in(key, 101), device_row_total, E_G2M)
    picked = jax.random.randint(jax.random.fold_in(key, 102), (device_row_total, E_G2M), 0, MESH_PER_DEVICE)
    return jnp.where(live_slots, picked, MESH_PER_DEVICE).reshape(-1).astype(jnp.int32)


def draw_mesh_receiver(key, part):
    device_row_total = MESH_EDGE_SLOTS // E_MESH
    live_slots = live_mask(jax.random.fold_in(key, 201), device_row_total, E_MESH)
    picked = jax.random.randint(jax.random.fold_in(key, 202), (device_row_total, E_MESH), 0, MESH_PER_DEVICE)
    return jnp.where(live_slots, picked, MESH_PER_DEVICE).reshape(-1).astype(jnp.int32)


def draw_mesh_sender(key, part):
    device_row_total = MESH_EDGE_SLOTS // E_MESH
    slot_numbers = jnp.arange(MESH_EDGE_SLOTS, dtype=jnp.int32)
    owning_device_ids = slot_numbers // E_MESH
    fullest_device = jax.random.randint(jax.random.fold_in(key, 301), (), 0, device_row_total)
    tallies = slot_tallies(jax.random.fold_in(key, 302), device_row_total, 8, NEAR_ROW_SLOTS, 4, fullest_device)
    adjacent_index, within_bounds = adjacent_slot(jax.random.fold_in(key, 303), owning_device_ids, 8, MESH_LATITUDES, tallies, NEAR_ROW_SLOTS)
    chooser = jax.random.randint(jax.random.fold_in(key, 304), (MESH_EDGE_SLOTS,), 0, 20)
    own_rows = jax.random.randint(jax.random.fold_in(key, 305), (MESH_EDGE_SLOTS,), 0, MESH_PER_DEVICE)
    far_base = MESH_PER_DEVICE + 8 * NEAR_ROW_SLOTS
    random_source = jax.random.randint(jax.random.fold_in(key, 306), (MESH_EDGE_SLOTS,), 0, device_row_total)
    opposite_source = (owning_device_ids + device_row_total // 2) % device_row_total
    coin = jax.random.randint(jax.random.fold_in(key, 307), (MESH_EDGE_SLOTS,), 0, 2)
    far_source = jnp.where(coin == 0, opposite_source, random_source)
    far_slot = jax.random.randint(jax.random.fold_in(key, 308), (MESH_EDGE_SLOTS,), 0, FAR_ROW_SLOTS)
    distant_rows = far_base + far_source * FAR_ROW_SLOTS + far_slot
    opposite_rows = far_base + opposite_source * FAR_ROW_SLOTS + far_slot
    near_rows = jnp.where(within_bounds, MESH_PER_DEVICE + adjacent_index, own_rows)
    final_output = jnp.where(chooser < 13, own_rows, jnp.where(chooser < 17, near_rows, distant_rows))
    starting_slot = fullest_device * E_MESH
    final_output = jnp.where(slot_numbers == starting_slot, far_base + device_row_total * FAR_ROW_SLOTS - 1, final_output)
    final_output = jnp.where(slot_numbers == starting_slot + 1, 0, final_output)
    final_output = jnp.where(slot_numbers == starting_slot + 2, MESH_PER_DEVICE + 5 * NEAR_ROW_SLOTS - 1, final_output)
    forced = jnp.logical_and(slot_numbers >= starting_slot + 3, slot_numbers < starting_slot + 6)
    final_output = jnp.where(forced, opposite_rows, final_output)
    return final_output.astype(jnp.int32)


def plant(values, stream_key, smallest, largest):
    longest = values.shape.index(max(values.shape))
    spots = []
    for shift in (0, 1):
        where = [jax.random.randint(jax.random.fold_in(stream_key, axis), (), 0, length) for axis, length in enumerate(values.shape)]
        where[longest] = (where[longest] + shift) % values.shape[longest]
        spots.append(tuple(where))
    return values.at[spots[0]].set(smallest).at[spots[1]].set(largest)


def block_scale(own_key, extent, cuts, low, largest):
    factor_of = 1.0
    for dim, shards_of in cuts:
        steps = jax.random.uniform(jax.random.fold_in(jax.random.fold_in(own_key, 6), dim), (shards_of,), jnp.float32, low / len(cuts), largest / len(cuts))
        factor_of = factor_of * jnp.repeat(jnp.exp(steps), extent[dim] // shards_of).reshape((-1,) + (1,) * (len(extent) - 1 - dim))
    return factor_of


def centred(key, shape, width, most, cuts=(), kind=jnp.bfloat16):
    values = jax.random.normal(key, shape, jnp.float32) * width
    if len(cuts) > 0:
        values = block_scale(key, shape, cuts, -0.22, 0.18) * values
    return jnp.clip(values, min=-most, max=most).astype(kind)


def setup_inputs(seed: int = 0) -> dict:
    streams_of = jax.random.split(jax.random.key(seed), 17)
    grid_feat = centred(streams_of[0], (GRID, C_IN), 1.0, 6.0, ((0, 32),))
    grid_send = plant(jax.random.randint(streams_of[1], (DEVICES, 4, GSLOT), 0, GRID_DEV), jax.random.fold_in(streams_of[1], 1), 0, GRID_DEV - 1).astype(jnp.int32)
    g2m_sender = draw_g2m_sender(jax.random.fold_in(streams_of[16], 71), 0)
    g2m_receiver = draw_g2m_receiver(jax.random.fold_in(streams_of[16], 71), 0)
    g2m_geom = jnp.clip(jax.random.uniform(streams_of[4], (4, G2M), jnp.float32, -1.0, 1.0) * block_scale(streams_of[4], (4, G2M), ((1, 32),), -0.4, 0.0), -1.0, 1.0)
    mesh_geom = jnp.clip(jax.random.uniform(streams_of[5], (3, MESH), jnp.float32, -1.0, 1.0) * block_scale(streams_of[5], (3, MESH), ((1, 32),), -0.4, 0.0), -1.0, 1.0)
    mesh_adjacent_lists = plant(jax.random.randint(streams_of[6], (DEVICES, 8, NEAR_ROW_SLOTS), 0, MESH_PER_DEVICE), jax.random.fold_in(streams_of[6], 1), 0, MESH_PER_DEVICE - 1).astype(jnp.int32)
    mesh_far = plant(jax.random.randint(streams_of[7], (DEVICES, DEVICES, FAR_ROW_SLOTS), 0, MESH_PER_DEVICE), jax.random.fold_in(streams_of[7], 1), 0, MESH_PER_DEVICE - 1).astype(jnp.int32)
    mesh_sender = draw_mesh_sender(jax.random.fold_in(streams_of[16], 71), 0)
    mesh_receiver = draw_mesh_receiver(jax.random.fold_in(streams_of[16], 71), 0)
    mesh_edge_geom = jnp.clip(jax.random.uniform(streams_of[10], (4, MESH_EDGE_SLOTS), jnp.float32, -1.0, 1.0) * block_scale(streams_of[10], (4, MESH_EDGE_SLOTS), ((1, 32),), -0.4, 0.0), -1.0, 1.0)
    embed_in = centred(streams_of[11], (C_IN, D), C_IN ** -0.5, 0.25)
    mesh_in = centred(streams_of[12], (3, D), 3 ** -0.5, 3.5, (), jnp.float32)
    geo_in = centred(streams_of[13], (SECTIONS, 4, D), 4 ** -0.5, 3.0, (), jnp.float32)
    pair_in = centred(streams_of[14], (SECTIONS, 4, D, D), (2 * D) ** -0.5, 0.1875)
    square_out = centred(streams_of[15], (SQUARES, D, D), D ** -0.5, 0.25)
    return {"grid_feat": grid_feat, "grid_send": grid_send, "g2m_sender": g2m_sender, "g2m_receiver": g2m_receiver, "g2m_geom": g2m_geom, "mesh_geom": mesh_geom, "mesh_adjacent_lists": mesh_adjacent_lists, "mesh_far": mesh_far, "mesh_sender": mesh_sender, "mesh_receiver": mesh_receiver, "mesh_edge_geom": mesh_edge_geom, "embed_in": embed_in, "mesh_in": mesh_in, "geo_in": geo_in, "pair_in": pair_in, "square_out": square_out}


EPSILON = 1e-05
GRID_OFFSETS = ((-1, 0), (1, 0), (0, -1), (0, 1))
MESH_OFFSETS = ((-1, -1), (-1, 0), (-1, 1), (0, -1), (0, 1), (1, -1), (1, 0), (1, 1))

def layer_norm(values):
    centre = values - lax.optimization_barrier(jnp.mean(values, axis=-1, keepdims=True))
    spread = lax.optimization_barrier(jnp.mean(centre * centre, axis=-1, keepdims=True))
    return centre * lax.rsqrt(spread + EPSILON)

def two_layer(pre_act, out_weight):
    hidden = jax.nn.silu(pre_act).astype(jnp.bfloat16)
    return layer_norm(jnp.dot(hidden, out_weight, preferred_element_type=jnp.float32))

def edge_sums(sender_term, receiver_term, senders, receivers, geometry, geo_weight, out_weight):
    node_count = receiver_term.shape[0]
    row_ids = jnp.minimum(receivers, node_count - 1)
    pre_act = jnp.dot(geometry.T, geo_weight, precision=lax.Precision.HIGHEST)
    pre_act = pre_act + sender_term[senders] + receiver_term[row_ids]
    message = two_layer(pre_act, out_weight).astype(jnp.bfloat16)
    summed = jax.ops.segment_sum(message.astype(jnp.float32), receivers, num_segments=node_count + 1)
    return summed[:node_count]

def node_update(latent, edge_sum, section_weights, out_weight):
    pre_act = jnp.dot(latent, section_weights[2], preferred_element_type=jnp.float32)
    pre_act = pre_act + jnp.dot(edge_sum.astype(jnp.bfloat16), section_weights[3], preferred_element_type=jnp.float32)
    return (latent.astype(jnp.float32) + two_layer(pre_act, out_weight)).astype(jnp.bfloat16)

def neighbour_rows(table, send_lists, device_id, offsets):
    lat_here = device_id // N_LON
    lon_here = device_id % N_LON
    gathered = []
    for offset_id, (lat_step, lon_step) in enumerate(offsets):
        source_lat = lat_here - lat_step
        source_lon = (lon_here - lon_step) % N_LON
        within_bounds = jnp.logical_and(source_lat >= 0, source_lat < N_LAT)
        source_id = (jnp.clip(source_lat, 0, N_LAT - 1) * N_LON + source_lon).astype(jnp.int32)
        rows = table[source_id][send_lists[source_id, offset_id]]
        gathered.append(jnp.where(within_bounds, rows, jnp.zeros_like(rows)))
    return gathered

def reference(grid_feat, grid_send, g2m_sender, g2m_receiver, g2m_geom, mesh_geom, mesh_adjacent_lists, mesh_far, mesh_sender, mesh_receiver, mesh_edge_geom, embed_in, mesh_in, geo_in, pair_in, square_out):
    device_row_total = N_LAT * N_LON
    source = jnp.arange(device_row_total, dtype=jnp.int32)[:, None]
    device_ids = jnp.arange(device_row_total, dtype=jnp.int32)

    def embed_rows(rows_in):
        pre_act = jnp.dot(rows_in, embed_in, preferred_element_type=jnp.float32)
        return two_layer(pre_act, square_out[0]).astype(jnp.bfloat16)
    grid_latent = lax.map(embed_rows, grid_feat.reshape(device_row_total, GRID_DEV, C_IN))

    def encode(inputs):
        device_id, senders, receivers, geometry, node_geo = inputs
        blocks = [grid_latent[device_id]] + neighbour_rows(grid_latent, grid_send, device_id, GRID_OFFSETS)
        received = jnp.concatenate(blocks, axis=0)
        sender_term = jnp.dot(received, pair_in[0, 0], preferred_element_type=jnp.float32)
        mesh_first = jnp.dot(node_geo.T, mesh_in, precision=lax.Precision.HIGHEST)
        mesh_start = two_layer(mesh_first, square_out[1]).astype(jnp.bfloat16)
        receiver_term = jnp.dot(mesh_start, pair_in[0, 1], preferred_element_type=jnp.float32)
        edge_sum = edge_sums(sender_term, receiver_term, senders, receivers, geometry, geo_in[0], square_out[2])
        return node_update(mesh_start, edge_sum, pair_in[0], square_out[3])
    mesh_latent = lax.map(encode, (device_ids, g2m_sender.reshape(device_row_total, E_G2M), g2m_receiver.reshape(device_row_total, E_G2M), g2m_geom.reshape(4, device_row_total, E_G2M).transpose(1, 0, 2), mesh_geom.reshape(3, device_row_total, MESH_PER_DEVICE).transpose(1, 0, 2)))
    edge_senders = mesh_sender.reshape(device_row_total, E_MESH)
    edge_receivers = mesh_receiver.reshape(device_row_total, E_MESH)
    edge_geometry = mesh_edge_geom.reshape(4, device_row_total, E_MESH).transpose(1, 0, 2)
    for section_id in range(1, STEPS + 1):

        def process(inputs, section_id=section_id, previous=mesh_latent):
            device_id, senders, receivers, geometry = inputs
            own_rows = previous[device_id]
            near_blocks = neighbour_rows(previous, mesh_adjacent_lists, device_id, MESH_OFFSETS)
            far_block = previous[source, mesh_far[:, device_id, :]].reshape(-1, D)
            sender_table = jnp.concatenate([own_rows] + near_blocks + [far_block], axis=0)
            sender_term = jnp.dot(sender_table, pair_in[section_id, 0], preferred_element_type=jnp.float32)
            receiver_term = jnp.dot(own_rows, pair_in[section_id, 1], preferred_element_type=jnp.float32)
            edge_sum = edge_sums(sender_term, receiver_term, senders, receivers, geometry, geo_in[section_id], square_out[2 + 2 * section_id])
            return node_update(own_rows, edge_sum, pair_in[section_id], square_out[3 + 2 * section_id])
        mesh_latent = lax.map(process, (device_ids, edge_senders, edge_receivers, edge_geometry))
    return mesh_latent.reshape(MESH, D)
```

```python
import functools

import jax
import jax.numpy as jnp
from jax import lax
from jax.experimental import pallas as pl
from jax.experimental.pallas import tpu as pltpu
from jax.sharding import PartitionSpec as P

EPSILON = 1e-05
TILE = 256
WINDOW = 256
LANES = 128
GEO_ROWS = 16
AXES = ("lat", "lon")
BF16 = jnp.bfloat16
F32 = jnp.float32
NT = (((1,), (1,)), ((), ()))


def up(n, m):
    return -(-n // m) * m


def mm(a, b):
    return jnp.dot(a, b, preferred_element_type=F32)


def mm_nt(a, b):
    return lax.dot_general(a, b, NT, preferred_element_type=F32)


def silu_bf16(x):
    half = 0.5 * x
    return (half + half * jnp.tanh(half)).astype(BF16)


def norm(values, axis):
    scale = 1.0 / values.shape[axis]
    centre = values - jnp.sum(values, axis=axis, keepdims=True) * scale
    spread = jnp.sum(centre * centre, axis=axis, keepdims=True) * scale
    return centre * lax.rsqrt(spread + EPSILON)


def one_hot_rows(ids, count):
    rows = lax.broadcasted_iota(jnp.int32, (count, ids.shape[1]), 0)
    return (rows == ids).astype(F32).astype(BF16)


def edge_tiles(first, last, lo_ref, hi_ref, key_ref, geo_ref, st_ref, rg_ref, wo_ref, acc_ref, pre_ref, shift):
    node_count = acc_ref.shape[0]

    def one_tile(tile, carry):
        lanes = pl.ds(pl.multiple_of(tile * TILE, TILE), TILE)
        key = key_ref[:, lanes]
        sender = lax.shift_right_logical(key, shift)
        receiver = key & ((1 << shift) - 1)
        incidence = one_hot_rows(receiver, node_count)
        base = (lo_ref[tile] // LANES) * LANES
        windows = (hi_ref[tile] - base) // WINDOW + 1

        def window(start):
            start = pl.multiple_of(start, LANES)
            return mm(st_ref[:, pl.ds(start, WINDOW)], one_hot_rows(sender - start, WINDOW))

        pre_ref[...] = mm(
            rg_ref[...], jnp.concatenate([incidence, geo_ref[:, lanes]], axis=0)
        ) + window(base)

        @pl.when(windows > 1)
        def _():
            def more(i, c):
                pre_ref[...] += window(base + i * WINDOW)
                return c

            lax.fori_loop(1, windows, more, 0)

        message = norm(mm(wo_ref[...], silu_bf16(pre_ref[...])), 0).astype(BF16)
        acc_ref[...] += mm_nt(incidence, message)
        return carry

    lax.fori_loop(first, last, one_tile, 0)


def pick_kernel(ids_ref, table_ref, out_ref):
    rows = table_ref.shape[0]
    for part in range(ids_ref.shape[0]):
        wide = jnp.broadcast_to(ids_ref[part : part + 1, :].astype(F32), (LANES, LANES))
        column = wide.T[:, :1].astype(jnp.int32)
        hot = (lax.broadcasted_iota(jnp.int32, (LANES, rows), 1) == column).astype(F32).astype(BF16)
        out_ref[part * LANES : (part + 1) * LANES, :] = mm(hot, table_ref[...]).astype(BF16)


def embed_grid(rows_ref, embed_ref, square_ref, wst_ref, st_ref, lane_offset):
    chunk = 256
    for part in range(rows_ref.shape[0] // chunk):
        hidden = silu_bf16(mm(rows_ref[part * chunk : (part + 1) * chunk, :], embed_ref[...]))
        latent = norm(mm(hidden, square_ref[0]), 1).astype(BF16)
        at = lane_offset + part * chunk
        st_ref[:, at : at + chunk] = mm_nt(wst_ref[...], latent).astype(BF16)


def fill_receivers(rg_ref, latent, weight_t, wg_ref):
    nodes = latent.shape[0]
    rg_ref[:, :nodes] = mm_nt(weight_t, latent).astype(BF16)
    rg_ref[:, nodes:] = wg_ref[0]


def first_encoder_kernel(shift, cut_ref, lo_ref, hi_ref, key_ref, geo_ref, grid_ref, mesh_geom_ref, embed_ref, mesh_in_ref,
                         square_grid_ref, square_mesh_ref, square_edge_ref, pair_ref, wg_ref,
                         st_ref, rg_ref, acc_ref, wst_ref, wo_ref, start_ref, pre_ref):
    wst_ref[...] = pair_ref[0, 0].T
    wo_ref[...] = square_edge_ref[0].T
    own = grid_ref.shape[0]
    st_ref[:, own:] = jnp.zeros((st_ref.shape[0], st_ref.shape[1] - own), BF16)
    embed_grid(grid_ref, embed_ref, square_grid_ref, wst_ref, st_ref, 0)
    geom = mesh_geom_ref[...]
    first = geom[:, 0:1] * mesh_in_ref[0:1, :]
    for k in range(1, geom.shape[1]):
        first = first + geom[:, k : k + 1] * mesh_in_ref[k : k + 1, :]
    start = norm(mm(silu_bf16(first), square_mesh_ref[0]), 1).astype(BF16)
    start_ref[...] = start
    fill_receivers(rg_ref, start, pair_ref[0, 1].T, wg_ref)
    acc_ref[...] = jnp.zeros_like(acc_ref)
    edge_tiles(0, cut_ref[0], lo_ref, hi_ref, key_ref, geo_ref, st_ref, rg_ref, wo_ref, acc_ref, pre_ref, shift)


def first_step_kernel(shift, cut_ref, lo_ref, hi_ref, key_ref, geo_ref, latent_ref, square_edge_ref, pair_ref, wg_ref,
                      st_ref, rg_ref, acc_ref, wst_ref, wo_ref, pre_ref):
    wst_ref[...] = pair_ref[0, 0].T
    wo_ref[...] = square_edge_ref[0].T
    own = latent_ref.shape[0]
    latent = latent_ref[...]
    st_ref[:, own:] = jnp.zeros((st_ref.shape[0], st_ref.shape[1] - own), BF16)
    st_ref[:, :own] = mm_nt(wst_ref[...], latent).astype(BF16)
    fill_receivers(rg_ref, latent, pair_ref[0, 1].T, wg_ref)
    acc_ref[...] = jnp.zeros_like(acc_ref)
    edge_tiles(0, cut_ref[0], lo_ref, hi_ref, key_ref, geo_ref, st_ref, rg_ref, wo_ref, acc_ref, pre_ref, shift)


def second_kernel(shift, own_pad, halo_count, encoder, last, cut_ref, lo_ref, hi_ref, key_ref, geo_ref, *refs):
    halo_refs, refs = refs[:halo_count], refs[halo_count:]
    if encoder:
        embed_ref, square_grid_ref, *refs = refs
    st_own_ref, rg_ref, acc_in_ref, wst_ref, wo_ref, latent_ref, pair_ref, square_node_ref, *refs = refs
    if last:
        out_ref, st_ref, acc_ref, pre_ref = refs
    else:
        ids_ref, out_ref, send_ref, st_ref, acc_ref, pre_ref = refs
    st_ref[:, :own_pad] = st_own_ref[:, :own_pad]
    at = own_pad
    for halo_ref in halo_refs:
        rows = halo_ref.shape[0]
        if encoder:
            embed_grid(halo_ref, embed_ref, square_grid_ref, wst_ref, st_ref, at)
        else:
            st_ref[:, at : at + rows] = mm_nt(wst_ref[...], halo_ref[...]).astype(BF16)
        at += rows
    st_ref[:, at:] = jnp.zeros((st_ref.shape[0], st_ref.shape[1] - at), BF16)
    acc_ref[...] = acc_in_ref[...]
    edge_tiles(cut_ref[0], key_ref.shape[1] // TILE, lo_ref, hi_ref, key_ref, geo_ref, st_ref, rg_ref, wo_ref, acc_ref, pre_ref, shift)
    latent = latent_ref[...]
    pre_act = mm(latent, pair_ref[0, 2]) + mm(acc_ref[...].astype(BF16), pair_ref[0, 3])
    new = (latent.astype(F32) + norm(mm(silu_bf16(pre_act), square_node_ref[0]), 1)).astype(BF16)
    out_ref[...] = new
    if not last:
        pick_kernel(ids_ref, out_ref, send_ref)


def whole(shape):
    return pl.BlockSpec(shape, lambda i: (0,) * len(shape))


def block_of(array, index):
    shape = (1,) + array.shape[1:]
    return pl.BlockSpec(shape, lambda i: (index,) + (0,) * (len(shape) - 1))


SMEM = pl.BlockSpec(memory_space=pltpu.SMEM)


def call(body, ins, outs, scratch=()):
    arrays = [a for a, _ in ins]
    specs = [whole(a.shape) if s is None else s for a, s in ins]
    return pl.pallas_call(
        body,
        grid=(1,),
        in_specs=specs,
        out_specs=[whole(o.shape) for o in outs],
        out_shape=outs,
        scratch_shapes=list(scratch),
        compiler_params=pltpu.CompilerParams(vmem_limit_bytes=48 * 1024 * 1024),
    )(*arrays)


def shaped(shape, dtype):
    return jax.ShapeDtypeStruct(shape, dtype)


def pair_route(parity, lon_step):
    n_lat, n_lon = lax.axis_size("lat"), lax.axis_size("lon")
    route = []
    for lat in range(n_lat):
        other = lat + 1 if lat % 2 == parity else lat - 1
        if 0 <= other < n_lat:
            route += [(lat * n_lon + (lon - lon_step) % n_lon, other * n_lon + lon) for lon in range(n_lon)]
    return route


def lon_route(parity):
    n_lat, n_lon = lax.axis_size("lat"), lax.axis_size("lon")
    route = []
    for lat in range(n_lat):
        for lon in range(n_lon):
            other = (lon + 1 if lon % 2 == parity else lon - 1) % n_lon
            route.append((lat * n_lon + lon, lat * n_lon + other))
    return route


def order_edges(position, receivers, geometry, own_pad, shift):
    edges = receivers.shape[0]
    key, *geo = lax.sort(((position << shift) | receivers, *geometry), num_keys=1)
    features = jnp.stack(geo, axis=0)
    high = lax.reduce_precision(features, 8, 7)
    low = features - high
    geo_rows = jnp.concatenate(
        [high, low, high, jnp.zeros((GEO_ROWS - 3 * len(geo), edges), F32)], axis=0
    ).astype(BF16)
    sender = key >> shift
    tiles = sender.reshape(-1, TILE)
    lo, hi = tiles[:, 0], tiles[:, -1]
    cut = jnp.sum((hi < own_pad).astype(jnp.int32)).reshape(1)
    return [(cut, SMEM), (lo, SMEM), (hi, SMEM), (key.reshape(1, edges), None), (geo_rows, None)]


def per_device(
    grid_feat,
    grid_send,
    g2m_sender,
    g2m_receiver,
    g2m_geom,
    mesh_geom,
    mesh_adjacent_lists,
    mesh_far,
    mesh_sender,
    mesh_receiver,
    mesh_edge_geom,
    embed_in,
    mesh_in,
    geo_in,
    pair_in,
    square_out,
):
    width = embed_in.shape[1]
    own_grid = grid_feat.shape[0]
    slot = grid_send.shape[2]
    nodes = mesh_geom.shape[1]
    near = mesh_adjacent_lists.shape[2]
    far = mesh_far.shape[1] * mesh_far.shape[2]
    edges = mesh_sender.shape[0]
    shift = nodes.bit_length()
    lat_odd = lax.axis_index("lat") % 2
    lon_odd = lax.axis_index("lon") % 2

    high = lax.reduce_precision(geo_in, 8, 7)
    geo_columns = jnp.concatenate(
        [high, high, geo_in - high, jnp.zeros((geo_in.shape[0], GEO_ROWS - 3 * geo_in.shape[1], width), F32)], axis=1
    ).transpose(0, 2, 1).astype(BF16)

    lists = grid_send[0]
    order = [
        jnp.where(lat_odd == 1, lists[1], lists[0]),
        jnp.where(lat_odd == 1, lists[0], lists[1]),
        jnp.where(lon_odd == 1, lists[3], lists[2]),
        jnp.where(lon_odd == 1, lists[2], lists[3]),
    ]
    ids = jnp.stack(order).reshape(-1, LANES)
    (outgoing,) = call(
        pick_kernel, [(ids, None), (grid_feat, None)], [shaped((4 * slot, grid_feat.shape[1]), BF16)]
    )
    routes = [pair_route(1, 0), pair_route(0, 0), lon_route(1), lon_route(0)]
    arrived = [lax.ppermute(outgoing[i * slot : (i + 1) * slot], AXES, r) for i, r in enumerate(routes)]

    grid_pad = up(own_grid, LANES)
    offset = g2m_sender - own_grid
    side = offset // slot
    lat_slot = jnp.where((side == 0) == (lat_odd == 0), 1, 0)
    lon_slot = jnp.where((side == 2) == (lon_odd == 0), 3, 2)
    grid_slot = jnp.where(side < 2, lat_slot, lon_slot)
    position = jnp.where(g2m_sender < own_grid, g2m_sender, grid_pad + grid_slot * slot + offset % slot)
    encoder_edges = order_edges(position, g2m_receiver, g2m_geom, grid_pad, shift)

    rg_width = nodes + GEO_ROWS
    square = lambda k: (square_out, block_of(square_out, k))
    pre_scratch = pltpu.VMEM((width, TILE), F32)
    acc_shape = shaped((nodes, width), F32)
    weight_shape = shaped((width, width), BF16)

    st, rg, acc, wst, wo, latent = call(
        functools.partial(first_encoder_kernel, shift),
        encoder_edges
        + [(grid_feat, None), (mesh_geom.T, None), (embed_in, None), (mesh_in, None), square(0), square(1), square(2),
           (pair_in, block_of(pair_in, 0)), (geo_columns, block_of(geo_columns, 0))],
        [shaped((width, grid_pad + LANES), BF16), shaped((width, rg_width), BF16), acc_shape, weight_shape, weight_shape,
         shaped((nodes, width), BF16)],
        [pre_scratch],
    )

    near_lists = mesh_adjacent_lists[0]
    ahead, behind, beside = near_lists[5:8], near_lists[0:3], near_lists[3:5]
    near_order = jnp.concatenate([
        jnp.where(lat_odd == 1, ahead, behind),
        jnp.where(lat_odd == 1, behind, ahead),
        jnp.where(lon_odd == 1, beside[1:2], beside[0:1]),
        jnp.where(lon_odd == 1, beside[0:1], beside[1:2]),
    ]).reshape(-1)
    send_ids = jnp.concatenate([near_order, mesh_far[0].reshape(-1)])
    send_pad = up(send_ids.shape[0], LANES)
    send_ids = jnp.pad(send_ids, (0, send_pad - send_ids.shape[0])).reshape(-1, LANES)
    mesh_routes = [pair_route(1, v) for v in (-1, 0, 1)] + [pair_route(0, v) for v in (-1, 0, 1)]
    mesh_routes += [lon_route(1), lon_route(0)]

    mesh_pad = up(nodes, LANES)
    offset = mesh_sender - nodes
    side = offset // near
    up_side = side >= 5
    lat_slot = jnp.where(up_side == (lat_odd == 1), 3, 0) + jnp.where(up_side, side - 5, side)
    lon_slot = jnp.where((side == 3) == (lon_odd == 0), 7, 6)
    near_slot = jnp.where((side == 3) | (side == 4), lon_slot, lat_slot)
    halo_row = jnp.where(offset < 8 * near, near_slot * near + offset % near, offset)
    position = jnp.where(mesh_sender < nodes, mesh_sender, mesh_pad + halo_row)
    mesh_edges = order_edges(position, mesh_receiver, mesh_edge_geom, mesh_pad, shift)

    sections = geo_in.shape[0]
    halos = arrived
    for section in range(sections):
        encoder, last = section == 0, section == sections - 1
        if section > 0:
            st, rg, acc, wst, wo = call(
                functools.partial(first_step_kernel, shift),
                mesh_edges
                + [(latent, None), square(2 + 2 * section), (pair_in, block_of(pair_in, section)),
                   (geo_columns, block_of(geo_columns, section))],
                [shaped((width, mesh_pad + LANES), BF16), shaped((width, rg_width), BF16), acc_shape, weight_shape, weight_shape],
                [pre_scratch],
            )
        own_pad = grid_pad if encoder else mesh_pad
        halo_rows = sum(h.shape[0] for h in halos)
        ins = (encoder_edges if encoder else mesh_edges) + [(h, None) for h in halos]
        if encoder:
            ins += [(embed_in, None), square(0)]
        ins += [(st, None), (rg, None), (acc, None), (wst, None), (wo, None), (latent, None),
                (pair_in, block_of(pair_in, section)), square(3 + 2 * section)]
        outs = [shaped((nodes, width), BF16)]
        if not last:
            ins += [(send_ids, None)]
            outs += [shaped((send_pad, width), BF16)]
        scratch = [pltpu.VMEM((width, own_pad + up(halo_rows, LANES) + LANES), BF16), pltpu.VMEM((nodes, width), F32), pre_scratch]
        out = call(
            functools.partial(second_kernel, shift, own_pad, len(halos), encoder, last), ins, outs, scratch
        )
        latent = out[0]
        if not last:
            send = out[1]
            far_out = send[8 * near : 8 * near + far].reshape(mesh_far.shape[1], -1, width)
            far_in = lax.all_to_all(far_out, AXES, split_axis=0, concat_axis=0, tiled=True)
            halos = [lax.ppermute(send[i * near : (i + 1) * near], AXES, r) for i, r in enumerate(mesh_routes)]
            halos = [jnp.concatenate(halos, axis=0), far_in.reshape(-1, width)]
    return latent


def solution(mesh):
    in_specs = (
        P(("lat", "lon"), None),
        P(("lat", "lon"), None, None),
        P(("lat", "lon")),
        P(("lat", "lon")),
        P(None, ("lat", "lon")),
        P(None, ("lat", "lon")),
        P(("lat", "lon"), None, None),
        P(("lat", "lon"), None, None),
        P(("lat", "lon")),
        P(("lat", "lon")),
        P(None, ("lat", "lon")),
        P(),
        P(),
        P(),
        P(),
        P(),
    )
    out_specs = P(("lat", "lon"), None)
    return jax.shard_map(
        per_device, mesh=mesh, in_specs=in_specs, out_specs=out_specs, check_vma=False
    )
```

```python
import functools

import jax
import jax.numpy as jnp
from jax import lax
from jax.experimental import pallas as pl
from jax.experimental.pallas import tpu as pltpu
from jax.sharding import PartitionSpec as P

EPSILON = 1e-05
TILE = 512
GROUP = 2
FIRST_WINDOW = 256
SECOND_WINDOW = 512
VMEM_LIMIT = 60 * 1024 * 1024
LANES = 128
GEO_ROWS = 16
AXES = ("lat", "lon")
BF16 = jnp.bfloat16
F32 = jnp.float32
NT = (((1,), (1,)), ((), ()))
TN = (((0,), (0,)), ((), ()))


def up(n, m):
    return -(-n // m) * m


def mm(a, b):
    return jnp.dot(a, b, preferred_element_type=F32)


def mm_nt(a, b):
    return lax.dot_general(a, b, NT, preferred_element_type=F32)


def silu_bf16(x):
    half = 0.5 * x
    return (half + half * jnp.tanh(half)).astype(BF16)


def norm(values, axis):
    scale = 1.0 / values.shape[axis]
    centre = values - jnp.sum(values, axis=axis, keepdims=True) * scale
    spread = jnp.sum(centre * centre, axis=axis, keepdims=True) * scale
    return centre * lax.rsqrt(spread + EPSILON)


def one_hot_rows(ids, count):
    rows = lax.broadcasted_iota(jnp.int32, (count, ids.shape[1]), 0)
    return (rows == ids).astype(F32).astype(BF16)


def last_sender(key_smem, tile, shift):
    return lax.shift_right_logical(key_smem[tile * TILE + TILE - 1], shift)


def own_tiles(key_smem, own_pad, shift):
    tiles = key_smem.shape[0] // TILE
    return lax.fori_loop(
        0, tiles, lambda t, c: c + (last_sender(key_smem, t, shift) < own_pad).astype(jnp.int32), jnp.int32(0)
    )


def split_rows(values, pattern):
    high = values.astype(BF16)
    low = (values - high.astype(F32)).astype(BF16)
    parts = [high if p == "h" else low for p in pattern]
    spare = GEO_ROWS - len(pattern) * values.shape[0]
    parts = [p.astype(F32) for p in parts] + [jnp.zeros((spare, values.shape[1]), F32)]
    return jnp.concatenate(parts, axis=0).astype(BF16)


def edge_tiles(first, last, window, shift, edge_refs, st_ref, rg_ref, wo_ref, acc_ref, pre_ref, mid_ref, inc_ref, more_ref):
    key_smem, key_ref, geo_ref = edge_refs
    node_count = acc_ref.shape[0]

    def tile_lanes(tile):
        return pl.ds(pl.multiple_of(tile * TILE, TILE), TILE)

    def base_of(tile):
        return (lax.shift_right_logical(key_smem[tile * TILE], shift) // LANES) * LANES

    def windows_of(tile):
        return (last_sender(key_smem, tile, shift) - base_of(tile)) // window + 1

    def sender_part(tile, start):
        sender = lax.shift_right_logical(key_ref[:, tile_lanes(tile)], shift)
        start = pl.multiple_of(start, LANES)
        return mm(st_ref[:, pl.ds(start, window)], one_hot_rows(sender - start, window))

    def load(tile, slot):
        incidence = one_hot_rows(key_ref[:, tile_lanes(tile)] & ((1 << shift) - 1), node_count)
        inc_ref[slot] = incidence
        features = jnp.concatenate([incidence, geo_ref[:, tile_lanes(tile)]], axis=0)
        pre_ref[slot] = mm(rg_ref[...], features) + sender_part(tile, base_of(tile)) + more_ref[slot]

    def middle(slot):
        mid_ref[slot] = mm(wo_ref[...], silu_bf16(pre_ref[slot]))

    def store(slot):
        acc_ref[...] += mm_nt(inc_ref[slot], norm(mid_ref[slot], 0).astype(BF16))

    def run(tile, count):
        for slot in range(count):

            @pl.when(windows_of(tile + slot) > 1)
            def _():
                def further(i, c):
                    more_ref[slot] += sender_part(tile + slot, base_of(tile + slot) + i * window)
                    return c

                lax.fori_loop(1, windows_of(tile + slot), further, 0)

        for stage in (lambda s: load(tile + s, s), middle, store):
            for slot in range(count):
                stage(slot)

        for slot in range(count):

            @pl.when(windows_of(tile + slot) > 1)
            def _():
                more_ref[slot] = jnp.zeros(more_ref.shape[1:], F32)

    def together(i, c):
        run(first + i * GROUP, GROUP)
        return c

    def alone(tile, c):
        run(tile, 1)
        return c

    more_ref[...] = jnp.zeros_like(more_ref)
    groups = (last - first) // GROUP
    lax.fori_loop(0, groups, together, 0)
    lax.fori_loop(first + groups * GROUP, last, alone, 0)


def pick_grid_kernel(ids_ref, table_ref, *out_refs):
    rows = table_ref.shape[1]
    for part, out_ref in enumerate(out_refs):
        hot = one_hot_rows(ids_ref[part : part + 1, :], rows)
        out_ref[...] = mm(table_ref[...], hot).astype(BF16)


def pick_rows(ids_ref, first, count, table):
    rows = []
    for part in range(up(count, LANES) // LANES):
        wide = jnp.broadcast_to(ids_ref[first + part : first + part + 1, :].astype(F32), (LANES, LANES))
        column = wide.T[:, :1].astype(jnp.int32)
        hot = (lax.broadcasted_iota(jnp.int32, (LANES, table.shape[0]), 1) == column).astype(F32).astype(BF16)
        rows.append(mm(hot, table).astype(BF16))
    return jnp.concatenate(rows, axis=0)[:count]


def embed_columns(columns, embed_t, square_t, wst):
    latent = norm(mm(square_t, silu_bf16(mm(embed_t, columns))), 0).astype(BF16)
    return mm(wst, latent).astype(BF16)


class Mover:
    def __init__(self, sems):
        self.sems, self.used, self.out = sems, 0, []

    def start(self, source, target):
        copy = pltpu.make_async_copy(source, target, self.sems.at[self.used])
        self.used += 1
        copy.start()
        return copy

    def store(self, source, target):
        self.out.append(self.start(source, target))

    def finish(self):
        for copy in self.out:
            copy.wait()


def first_kernel(shift, section, own_pad, key_smem, *refs):
    refs = list(refs)
    take = lambda n: [refs.pop(0) for _ in range(n)]
    encoder = section == 0
    key_in, *geo_in = take(5)
    wg_in, square_in, pair_in = take(3)
    if encoder:
        grid_in, mesh_geom_in, embed_in, mesh_in = take(4)
    else:
        (latent_in,) = take(1)
    st_out, rg_out, acc_out, wst_out, wo_out, geo_out = take(6)
    if encoder:
        start_out, embed_t_out, square_t_out = take(3)
    sems, st_ref, rg_ref, acc_ref, wst_ref, wo_ref, latent_ref, key_ref, raw_ref, geo_ref, wg_ref, slots_ref = take(12)
    if encoder:
        grid_ref, mesh_geom_ref, embed_ref, mesh_in_ref, embed_t_ref, square_t_ref = take(6)
    stages = refs
    mover = Mover(sems)
    if encoder:
        embed_here = mover.start(embed_in, embed_ref)
        square_here = mover.start(square_in.at[0], slots_ref.at[3])
        grid_here = mover.start(grid_in, grid_ref)
    else:
        latent_here = mover.start(latent_in, latent_ref)
    sender_here = mover.start(pair_in.at[section, 0], slots_ref.at[0])
    if encoder:
        mesh_geom_here = mover.start(mesh_geom_in, mesh_geom_ref)
        mesh_in_here = mover.start(mesh_in, mesh_in_ref)
        square_mesh_here = mover.start(square_in.at[1], slots_ref.at[4])
    receiver_here = mover.start(pair_in.at[section, 1], slots_ref.at[1])
    wg_here = mover.start(wg_in.at[section], wg_ref)
    edge_here = mover.start(square_in.at[2 + 2 * section], slots_ref.at[2])
    key_here = mover.start(key_in, key_ref)
    geo_here = [mover.start(g, raw_ref.at[pl.ds(i, 1)]) for i, g in enumerate(geo_in)]

    acc_ref[...] = jnp.zeros_like(acc_ref)
    own = grid_ref.shape[1] if encoder else latent_ref.shape[0]
    st_ref[:, own:] = jnp.zeros((st_ref.shape[0], st_ref.shape[1] - own), BF16)
    if encoder:
        embed_here.wait()
        embed_t_ref[...] = embed_ref[...].T
        mover.store(embed_t_ref, embed_t_out)
        square_here.wait()
        square_t_ref[...] = slots_ref[3].T
        mover.store(square_t_ref, square_t_out)
    sender_here.wait()
    wst_ref[...] = slots_ref[0].T
    mover.store(wst_ref, wst_out)
    if encoder:
        grid_here.wait()
        st_ref[:, :own] = embed_columns(grid_ref[...], embed_t_ref[...], square_t_ref[...], wst_ref[...])
        mover.store(st_ref, st_out)
        mesh_geom_here.wait()
        mesh_in_here.wait()
        first = lax.dot_general(
            split_rows(mesh_geom_ref[...], "hlh"), split_rows(mesh_in_ref[...], "hhl"), TN, preferred_element_type=F32
        )
        square_mesh_here.wait()
        latent_ref[...] = norm(mm(silu_bf16(first), slots_ref[4]), 1).astype(BF16)
        mover.store(latent_ref, start_out)
    else:
        latent_here.wait()
        st_ref[:, :own] = mm_nt(wst_ref[...], latent_ref[...]).astype(BF16)
        mover.store(st_ref, st_out)
    receiver_here.wait()
    wg_here.wait()
    nodes = latent_ref.shape[0]
    rg_ref[:, :nodes] = mm_nt(slots_ref[1].T, latent_ref[...]).astype(BF16)
    rg_ref[:, nodes:] = split_rows(wg_ref[...], "hhl").T
    mover.store(rg_ref, rg_out)
    edge_here.wait()
    wo_ref[...] = slots_ref[2].T
    mover.store(wo_ref, wo_out)
    key_here.wait()
    for copy in geo_here:
        copy.wait()
    geo_ref[...] = split_rows(raw_ref[...], "hlh")
    mover.store(geo_ref, geo_out)
    edge_tiles(0, own_tiles(key_smem, own_pad, shift), FIRST_WINDOW, shift, (key_smem, key_ref, geo_ref), st_ref, rg_ref, wo_ref,
               acc_ref, *stages)
    mover.store(acc_ref, acc_out)
    mover.finish()


def second_kernel(shift, section, own_pad, halo_rows, send_counts, key_smem, *refs):
    refs = list(refs)
    take = lambda n: [refs.pop(0) for _ in range(n)]
    encoder = section == 0
    key_in, square_in, pair_in, st_in, rg_in, acc_in, wst_in, wo_in, geo_in, latent_in = take(10)
    halos_in = take(len(halo_rows))
    if encoder:
        embed_t_in, square_t_in = take(2)
    if send_counts:
        (ids_in,) = take(1)
    (new_out,) = take(1)
    sends_out = take(len(send_counts))
    sems, st_ref, rg_ref, acc_ref, wst_ref, wo_ref, latent_ref, key_ref, geo_ref, slots_ref, halo_ref, new_ref = take(12)
    if encoder:
        embed_t_ref, square_t_ref = take(2)
    if send_counts:
        (ids_ref,) = take(1)
        sends_ref = take(len(send_counts))
    stages = refs
    mover = Mover(sems)
    halos_here, at = [], 0
    for ref, rows in zip(halos_in, halo_rows):
        if encoder:
            halos_here.append(mover.start(ref, halo_ref.at[:, pl.ds(at, rows)]))
        else:
            halos_here.append(mover.start(ref.at[pl.ds(0, rows)], halo_ref.at[pl.ds(at, rows)]))
        at += rows
    if encoder:
        halos_here += [mover.start(embed_t_in, embed_t_ref), mover.start(square_t_in, square_t_ref)]
    halos_here.append(mover.start(wst_in, wst_ref))
    tables_here = [
        mover.start(st_in.at[:, pl.ds(0, own_pad)], st_ref.at[:, pl.ds(0, own_pad)]),
        mover.start(rg_in, rg_ref),
        mover.start(wo_in, wo_ref),
        mover.start(key_in, key_ref),
        mover.start(geo_in, geo_ref),
        mover.start(acc_in, acc_ref),
    ]
    late_here = [
        mover.start(latent_in, latent_ref),
        mover.start(pair_in.at[section, 2], slots_ref.at[0]),
        mover.start(pair_in.at[section, 3], slots_ref.at[1]),
        mover.start(square_in.at[3 + 2 * section], slots_ref.at[2]),
    ]
    if send_counts:
        late_here.append(mover.start(ids_in, ids_ref))
    total = halo_ref.shape[1] if encoder else halo_ref.shape[0]
    st_ref[:, own_pad + total :] = jnp.zeros((st_ref.shape[0], st_ref.shape[1] - own_pad - total), BF16)
    if not encoder and at < total:
        halo_ref[at:, :] = jnp.zeros((total - at, halo_ref.shape[1]), BF16)
    for copy in halos_here:
        copy.wait()
    if encoder:
        columns = embed_columns(halo_ref[...], embed_t_ref[...], square_t_ref[...], wst_ref[...])
    else:
        columns = mm_nt(wst_ref[...], halo_ref[...]).astype(BF16)
    st_ref[:, own_pad : own_pad + total] = columns
    for copy in tables_here:
        copy.wait()
    edge_tiles(own_tiles(key_smem, own_pad, shift), key_ref.shape[1] // TILE, SECOND_WINDOW, shift,
               (key_smem, key_ref, geo_ref), st_ref, rg_ref, wo_ref, acc_ref, *stages)
    for copy in late_here:
        copy.wait()
    latent = latent_ref[...]
    pre_act = mm(latent, slots_ref[0]) + mm(acc_ref[...].astype(BF16), slots_ref[1])
    new = (latent.astype(F32) + norm(mm(silu_bf16(pre_act), slots_ref[2]), 1)).astype(BF16)
    new_ref[...] = new
    mover.store(new_ref, new_out)
    if send_counts:
        at = 0
        for send_ref, send_out, count in zip(sends_ref, sends_out, send_counts):
            send_ref[...] = pick_rows(ids_ref, at, count, new)
            mover.store(send_ref, send_out)
            at += up(count, LANES) // LANES
    mover.finish()


SMEM = pl.BlockSpec(memory_space=pltpu.SMEM)
VMEM = pl.BlockSpec(memory_space=pltpu.VMEM)
ANY = pl.BlockSpec(memory_space=pl.ANY)


def call(body, ins, outs, scratch=(), flops=0, first=SMEM, rest=ANY):
    moved = sum(a.size * a.dtype.itemsize for a in outs)
    return pl.pallas_call(
        body,
        in_specs=[first] + [rest] * (len(ins) - 1),
        out_specs=[rest] * len(outs),
        out_shape=outs,
        scratch_shapes=list(scratch),
        compiler_params=pltpu.CompilerParams(vmem_limit_bytes=VMEM_LIMIT),
        cost_estimate=pl.CostEstimate(flops=flops, bytes_accessed=2 * moved, transcendentals=0),
    )(*ins)


def room(*arrays):
    return [pltpu.VMEM(a.shape, a.dtype) for a in arrays]


def room_for(mover_count):
    return [pltpu.SemaphoreType.DMA((mover_count,))]


def shaped(shape, dtype):
    return jax.ShapeDtypeStruct(shape, dtype)


def pair_route(parity, lon_step):
    n_lat, n_lon = lax.axis_size("lat"), lax.axis_size("lon")
    route = []
    for lat in range(n_lat):
        other = lat + 1 if lat % 2 == parity else lat - 1
        if 0 <= other < n_lat:
            route += [(lat * n_lon + (lon - lon_step) % n_lon, other * n_lon + lon) for lon in range(n_lon)]
    return route


def lon_route(parity):
    n_lat, n_lon = lax.axis_size("lat"), lax.axis_size("lon")
    route = []
    for lat in range(n_lat):
        for lon in range(n_lon):
            other = (lon + 1 if lon % 2 == parity else lon - 1) % n_lon
            route.append((lat * n_lon + lon, lat * n_lon + other))
    return route


def order_edges(position, receivers, geometry, shift):
    edges = receivers.shape[0]
    key, *geo = lax.sort(((position << shift) | receivers, *geometry), num_keys=1, is_stable=False)
    return (key,) + tuple(x.reshape(1, edges) for x in (key, *geo))


def per_device(
    grid_feat,
    grid_send,
    g2m_sender,
    g2m_receiver,
    g2m_geom,
    mesh_geom,
    mesh_adjacent_lists,
    mesh_far,
    mesh_sender,
    mesh_receiver,
    mesh_edge_geom,
    embed_in,
    mesh_in,
    geo_in,
    pair_in,
    square_out,
):
    width = embed_in.shape[1]
    own_grid = grid_feat.shape[0]
    slot = grid_send.shape[2]
    nodes = mesh_geom.shape[1]
    near = mesh_adjacent_lists.shape[2]
    far = mesh_far.shape[1] * mesh_far.shape[2]
    edges = mesh_sender.shape[0]
    shift = nodes.bit_length()
    lat_odd = lax.axis_index("lat") % 2
    lon_odd = lax.axis_index("lon") % 2

    lists = grid_send[0]
    ids = jnp.stack([
        jnp.where(lat_odd == 1, lists[1], lists[0]),
        jnp.where(lat_odd == 1, lists[0], lists[1]),
        jnp.where(lon_odd == 1, lists[3], lists[2]),
        jnp.where(lon_odd == 1, lists[2], lists[3]),
    ])
    grid_t = grid_feat.T
    outgoing = call(
        pick_grid_kernel, [ids, grid_t], [shaped((grid_t.shape[0], slot), BF16)] * 4, first=VMEM, rest=VMEM
    )
    routes = [pair_route(1, 0), pair_route(0, 0), lon_route(1), lon_route(0)]
    arrived = [lax.ppermute(rows, AXES, r) for rows, r in zip(outgoing, routes)]

    grid_pad = up(own_grid, LANES)
    offset = g2m_sender - own_grid
    side = offset // slot
    lat_slot = jnp.where((side == 0) == (lat_odd == 0), 1, 0)
    lon_slot = jnp.where((side == 2) == (lon_odd == 0), 3, 2)
    grid_slot = jnp.where(side < 2, lat_slot, lon_slot)
    position = jnp.where(g2m_sender < own_grid, g2m_sender, grid_pad + grid_slot * slot + offset % slot)
    encoder_edges = order_edges(position, g2m_receiver, g2m_geom, shift)

    rg_width = nodes + GEO_ROWS
    weights = [square_out, pair_in]
    tile_shape = (GROUP, width, TILE)
    stages = [pltpu.VMEM(tile_shape, F32)] * 2 + [pltpu.VMEM((GROUP, nodes, TILE), BF16), pltpu.VMEM(tile_shape, F32)]

    acc_shape = shaped((nodes, width), F32)
    latent_shape = shaped((nodes, width), BF16)
    rg_shape = shaped((width, rg_width), BF16)
    weight_shape = shaped((width, width), BF16)
    embed_t_shape = shaped(embed_in.shape[::-1], BF16)
    edge_flops = 2 * edges * width * (2 * width + 2 * nodes)

    geo_shape = shaped((GEO_ROWS, edges), BF16)
    raw_shape = shaped((geo_in.shape[1], edges), F32)

    def first_call(section, edge_arrays, own_pad, extra):
        table = shaped((width, own_pad + FIRST_WINDOW), BF16)
        outs = [table, rg_shape, acc_shape, weight_shape, weight_shape, geo_shape]
        held = outs[:5] + [latent_shape, edge_arrays[1], raw_shape, geo_shape, shaped(geo_in.shape[1:], F32),
                           shaped((5, width, width), BF16)]
        if section == 0:
            outs = outs + [latent_shape, embed_t_shape, weight_shape]
            held = held + list(extra) + [embed_t_shape, weight_shape]
        return call(
            functools.partial(first_kernel, shift, section, own_pad),
            list(edge_arrays) + [geo_in] + weights + list(extra),
            outs,
            room_for(32) + room(*held) + stages,
            edge_flops,
        )

    st, rg, acc, wst, wo, geo, latent, embed_t, square_t = first_call(
        0, encoder_edges, grid_pad, [grid_t, mesh_geom, embed_in, mesh_in]
    )

    near_lists = mesh_adjacent_lists[0]

    def lat_lists(first):
        left, centre, right = near_lists[first], near_lists[first + 1], near_lists[first + 2]
        return [centre, jnp.where(lon_odd == 1, left, right), jnp.where(lon_odd == 1, right, left)]

    ahead, behind = jnp.concatenate(lat_lists(5)), jnp.concatenate(lat_lists(0))
    sends = [
        jnp.where(lat_odd == 1, ahead, behind),
        jnp.where(lat_odd == 1, behind, ahead),
        jnp.where(lon_odd == 1, near_lists[3], near_lists[4]),
        jnp.where(lon_odd == 1, near_lists[4], near_lists[3]),
        mesh_far[0].reshape(-1),
    ]
    send_counts = tuple(ids.shape[0] for ids in sends)
    send_ids = jnp.concatenate(
        [jnp.pad(ids, (0, up(ids.shape[0], LANES) - ids.shape[0])).reshape(-1, LANES) for ids in sends]
    )
    odd_even, even_odd = pair_route(1, 0), pair_route(0, 0)
    mate, other = lon_route(0), lon_route(1)

    mesh_pad = up(nodes, LANES)
    offset = mesh_sender - nodes
    side = offset // near
    lat_step = jnp.where(side < 3, -1, jnp.where(side < 5, 0, 1))
    lon_step = jnp.where(side < 3, side - 1, jnp.where(side < 5, 2 * side - 7, side - 6))
    by_even = ((lat_step == 1) == (lat_odd == 1)).astype(jnp.int32)
    by_other = ((lon_step == -1) == (lon_odd == 1)).astype(jnp.int32)
    near_slot = jnp.where(
        lat_step == 0, by_other, jnp.where(lon_step == 0, 2 + by_even, 4 + 2 * by_even + by_other)
    )
    halo_row = jnp.where(offset < 8 * near, near_slot * near + offset % near, offset)
    position = jnp.where(mesh_sender < nodes, mesh_sender, mesh_pad + halo_row)
    mesh_edges = order_edges(position, mesh_receiver, mesh_edge_geom, shift)

    sections = geo_in.shape[0]
    halos = arrived
    for section in range(sections):
        encoder, last = section == 0, section == sections - 1
        if encoder:
            own_pad, halo_rows, halo_total = grid_pad, (slot,) * 4, up(4 * slot, LANES)
            smem_key, key = encoder_edges[:2]
            halo_shape = shaped((grid_t.shape[0], halo_total), BF16)
        else:
            own_pad, halo_rows, halo_total = mesh_pad, (near,) * 8 + (far,), up(8 * near + far, LANES)
            smem_key, key = mesh_edges[:2]
            halo_shape = shaped((halo_total, width), BF16)
        ins = [smem_key, key] + weights + [st, rg, acc, wst, wo, geo, latent] + list(halos)
        table = shaped((width, own_pad + halo_total + SECOND_WINDOW), BF16)
        held = [table, rg, acc_shape, weight_shape, weight_shape, latent_shape, key, geo_shape, shaped((3, width, width), BF16),
                halo_shape, latent_shape]
        if encoder:
            ins += [embed_t, square_t]
            held += [embed_t_shape, weight_shape]
        counts = () if last else send_counts
        outs = [latent_shape] + [shaped((count, width), BF16) for count in counts]
        if counts:
            ins += [send_ids]
            held += [send_ids] + outs[1:]
        out = call(
            functools.partial(second_kernel, shift, section, own_pad, halo_rows, counts),
            ins,
            outs,
            room_for(36) + room(*held) + stages,
            edge_flops,
        )
        latent = out[0]
        if not last:
            by_odd, by_even, to_mate, to_other, far_out = out[1:]
            by_odd = lax.ppermute(by_odd, AXES, odd_even)
            by_even = lax.ppermute(by_even, AXES, even_odd)
            far_out = far_out.reshape(mesh_far.shape[1], -1, width)
            to_pass = [by_odd[near : 2 * near], by_odd[2 * near :]]
            latent, *to_pass = lax.optimization_barrier((latent, *to_pass))
            far_in = lax.all_to_all(far_out, AXES, split_axis=0, concat_axis=0, tiled=True)
            to_mate, to_other = lax.ppermute(to_mate, AXES, mate), lax.ppermute(to_other, AXES, other)
            passed = [lax.ppermute(to_pass[0], AXES, mate), lax.ppermute(to_pass[1], AXES, other)]
            st, rg, acc, wst, wo, geo = first_call(section + 1, mesh_edges, mesh_pad, [latent])
            by_even, acc, far_in = lax.optimization_barrier((by_even, acc, far_in))
            passed += [lax.ppermute(by_even[near : 2 * near], AXES, mate), lax.ppermute(by_even[2 * near :], AXES, other)]
            halos = [to_mate, to_other, by_odd, by_even] + passed
            halos += [far_in.reshape(-1, width)]
    return latent


def solution(mesh):
    in_specs = (
        P(("lat", "lon"), None),
        P(("lat", "lon"), None, None),
        P(("lat", "lon")),
        P(("lat", "lon")),
        P(None, ("lat", "lon")),
        P(None, ("lat", "lon")),
        P(("lat", "lon"), None, None),
        P(("lat", "lon"), None, None),
        P(("lat", "lon")),
        P(("lat", "lon")),
        P(None, ("lat", "lon")),
        P(),
        P(),
        P(),
        P(),
        P(),
    )
    out_specs = P(("lat", "lon"), None)
    return jax.shard_map(
        per_device, mesh=mesh, in_specs=in_specs, out_specs=out_specs, check_vma=False
    )
```

```python
import functools

import jax
import jax.numpy as jnp
from jax import lax
from jax.experimental import pallas as pl
from jax.experimental.pallas import tpu as pltpu
from jax.sharding import PartitionSpec as P

EPSILON = 1e-05
TILE = 512
GROUP = 2
FIRST_WINDOW = 256
SECOND_WINDOW = 512
VMEM_LIMIT = 60 * 1024 * 1024
LANES = 128
GEO_ROWS = 16
AXES = ("lat", "lon")
BF16 = jnp.bfloat16
F32 = jnp.float32
NT = (((1,), (1,)), ((), ()))
TN = (((0,), (0,)), ((), ()))


def up(n, m):
    return -(-n // m) * m


def mm(a, b):
    return jnp.dot(a, b, preferred_element_type=F32)


def mm_nt(a, b):
    return lax.dot_general(a, b, NT, preferred_element_type=F32)


def silu_bf16(x):
    half = 0.5 * x
    return (half + half * jnp.tanh(half)).astype(BF16)


def norm(values, axis):
    scale = 1.0 / values.shape[axis]
    centre = values - jnp.sum(values, axis=axis, keepdims=True) * scale
    spread = jnp.sum(centre * centre, axis=axis, keepdims=True) * scale
    return centre * lax.rsqrt(spread + EPSILON)


def one_hot_rows(ids, count):
    rows = lax.broadcasted_iota(jnp.int32, (count, ids.shape[1]), 0)
    return (rows == ids).astype(F32).astype(BF16)


def last_sender(key_smem, tile, shift):
    return lax.shift_right_logical(key_smem[tile * TILE + TILE - 1], shift)


def own_tiles(key_smem, own_pad, shift):
    tiles = key_smem.shape[0] // TILE
    return lax.fori_loop(
        0, tiles, lambda t, c: c + (last_sender(key_smem, t, shift) < own_pad).astype(jnp.int32), jnp.int32(0)
    )


def split_rows(values, pattern):
    high = values.astype(BF16)
    low = (values - high.astype(F32)).astype(BF16)
    parts = [high if p == "h" else low for p in pattern]
    spare = GEO_ROWS - len(pattern) * values.shape[0]
    parts = [p.astype(F32) for p in parts] + [jnp.zeros((spare, values.shape[1]), F32)]
    return jnp.concatenate(parts, axis=0).astype(BF16)


def edge_tiles(first, last, window, shift, edge_refs, st_ref, rg_ref, wo_ref, acc_ref, pre_ref, mid_ref, inc_ref, more_ref):
    key_smem, key_ref, geo_ref = edge_refs
    node_count = acc_ref.shape[0]

    def tile_lanes(tile):
        return pl.ds(pl.multiple_of(tile * TILE, TILE), TILE)

    def base_of(tile):
        return (lax.shift_right_logical(key_smem[tile * TILE], shift) // LANES) * LANES

    def windows_of(tile):
        return (last_sender(key_smem, tile, shift) - base_of(tile)) // window + 1

    def sender_part(tile, start):
        sender = lax.shift_right_logical(key_ref[:, tile_lanes(tile)], shift)
        start = pl.multiple_of(start, LANES)
        return mm(st_ref[:, pl.ds(start, window)], one_hot_rows(sender - start, window))

    def load(tile, slot):
        incidence = one_hot_rows(key_ref[:, tile_lanes(tile)] & ((1 << shift) - 1), node_count)
        inc_ref[slot] = incidence
        features = jnp.concatenate([incidence, geo_ref[:, tile_lanes(tile)]], axis=0)
        pre_ref[slot] = mm(rg_ref[...], features) + sender_part(tile, base_of(tile)) + more_ref[slot]

    def middle(slot):
        mid_ref[slot] = mm(wo_ref[...], silu_bf16(pre_ref[slot]))

    def store(slot):
        acc_ref[...] += mm_nt(inc_ref[slot], norm(mid_ref[slot], 0).astype(BF16))

    def run(tile, count):
        for slot in range(count):

            @pl.when(windows_of(tile + slot) > 1)
            def _():
                def further(i, c):
                    more_ref[slot] += sender_part(tile + slot, base_of(tile + slot) + i * window)
                    return c

                lax.fori_loop(1, windows_of(tile + slot), further, 0)

        for stage in (lambda s: load(tile + s, s), middle, store):
            for slot in range(count):
                stage(slot)

        for slot in range(count):

            @pl.when(windows_of(tile + slot) > 1)
            def _():
                more_ref[slot] = jnp.zeros(more_ref.shape[1:], F32)

    def together(i, c):
        run(first + i * GROUP, GROUP)
        return c

    def alone(tile, c):
        run(tile, 1)
        return c

    more_ref[...] = jnp.zeros_like(more_ref)
    groups = (last - first) // GROUP
    lax.fori_loop(0, groups, together, 0)
    lax.fori_loop(first + groups * GROUP, last, alone, 0)


def pick_rows(ids_ref, first, count, table):
    rows = []
    for part in range(up(count, LANES) // LANES):
        wide = jnp.broadcast_to(ids_ref[first + part : first + part + 1, :].astype(F32), (LANES, LANES))
        column = wide.T[:, :1].astype(jnp.int32)
        hot = (lax.broadcasted_iota(jnp.int32, (LANES, table.shape[0]), 1) == column).astype(F32).astype(BF16)
        rows.append(mm(hot, table).astype(BF16))
    return jnp.concatenate(rows, axis=0)[:count]


class Mover:
    def __init__(self, sems):
        self.sems, self.used, self.out = sems, 0, []

    def start(self, source, target):
        copy = pltpu.make_async_copy(source, target, self.sems.at[self.used])
        self.used += 1
        copy.start()
        return copy

    def store(self, source, target):
        self.out.append(self.start(source, target))

    def finish(self):
        for copy in self.out:
            copy.wait()


def grid_kernel(ids_in, grid_in, embed_in, square_in, pair_in, st_out, *refs):
    refs = list(refs)
    take = lambda n: [refs.pop(0) for _ in range(n)]
    sends_out = take(4)
    sems, ids_ref, grid_ref, embed_ref, slots_ref, st_ref = take(6)
    sends_ref = refs
    mover = Mover(sems)
    embed_here = mover.start(embed_in, embed_ref)
    grid_here = mover.start(grid_in, grid_ref)
    square_here = mover.start(square_in.at[0], slots_ref.at[0])
    sender_here = mover.start(pair_in.at[0, 0], slots_ref.at[1])
    ids_here = mover.start(ids_in, ids_ref)
    own = grid_ref.shape[1]
    st_ref[:, own:] = jnp.zeros((st_ref.shape[0], st_ref.shape[1] - own), BF16)
    embed_here.wait()
    embed_t = embed_ref[...].T
    grid_here.wait()
    hidden = silu_bf16(mm(embed_t, grid_ref[...]))
    square_here.wait()
    latent = norm(mm(slots_ref[0].T, hidden), 0).astype(BF16)
    sender_here.wait()
    st_ref[:, :own] = mm(slots_ref[1].T, latent).astype(BF16)
    mover.store(st_ref, st_out)
    ids_here.wait()
    lat_odd = lax.axis_index("lat") % 2 == 1
    lon_odd = lax.axis_index("lon") % 2 == 1
    ids = [ids_ref[i : i + 1, :] for i in range(4)]
    asked = [
        jnp.where(lat_odd, ids[1], ids[0]),
        jnp.where(lat_odd, ids[0], ids[1]),
        jnp.where(lon_odd, ids[3], ids[2]),
        jnp.where(lon_odd, ids[2], ids[3]),
    ]
    for wanted, send_ref, send_out in zip(asked, sends_ref, sends_out):
        send_ref[...] = mm(st_ref[:, :own], one_hot_rows(wanted, own)).astype(BF16)
        mover.store(send_ref, send_out)
    mover.finish()


def first_kernel(shift, section, own_pad, key_smem, *refs):
    refs = list(refs)
    take = lambda n: [refs.pop(0) for _ in range(n)]
    encoder = section == 0
    key_in, *geo_in = take(5)
    wg_in, square_in, pair_in = take(3)
    if encoder:
        st_in, mesh_geom_in, mesh_in = take(3)
    else:
        (latent_in,) = take(1)
    rg_out, acc_out, wo_out, geo_out = take(4)
    if encoder:
        (start_out,) = take(1)
    else:
        st_out, wst_out = take(2)
    sems, st_ref, rg_ref, acc_ref, wst_ref, wo_ref, latent_ref, key_ref, raw_ref, geo_ref, wg_ref, slots_ref = take(12)
    if encoder:
        mesh_geom_ref, mesh_in_ref = take(2)
    stages = refs
    mover = Mover(sems)
    if encoder:
        mesh_geom_here = mover.start(mesh_geom_in, mesh_geom_ref)
        mesh_in_here = mover.start(mesh_in, mesh_in_ref)
        square_mesh_here = mover.start(square_in.at[1], slots_ref.at[0])
    else:
        latent_here = mover.start(latent_in, latent_ref)
        sender_here = mover.start(pair_in.at[section, 0], slots_ref.at[0])
    receiver_here = mover.start(pair_in.at[section, 1], slots_ref.at[1])
    wg_here = mover.start(wg_in.at[section], wg_ref)
    edge_here = mover.start(square_in.at[2 + 2 * section], slots_ref.at[2])
    key_here = mover.start(key_in, key_ref)
    geo_here = [mover.start(g, raw_ref.at[pl.ds(i, 1)]) for i, g in enumerate(geo_in)]

    table_here = mover.start(st_in, st_ref) if encoder else None

    acc_ref[...] = jnp.zeros_like(acc_ref)
    if encoder:
        mesh_geom_here.wait()
        mesh_in_here.wait()
        first = lax.dot_general(
            split_rows(mesh_geom_ref[...], "hlh"), split_rows(mesh_in_ref[...], "hhl"), TN, preferred_element_type=F32
        )
        square_mesh_here.wait()
        latent_ref[...] = norm(mm(silu_bf16(first), slots_ref[0]), 1).astype(BF16)
        mover.store(latent_ref, start_out)
    else:
        own = latent_ref.shape[0]
        st_ref[:, own:] = jnp.zeros((st_ref.shape[0], st_ref.shape[1] - own), BF16)
        sender_here.wait()
        wst_ref[...] = slots_ref[0].T
        mover.store(wst_ref, wst_out)
        latent_here.wait()
        st_ref[:, :own] = mm_nt(wst_ref[...], latent_ref[...]).astype(BF16)
        mover.store(st_ref, st_out)
    receiver_here.wait()
    wg_here.wait()
    nodes = latent_ref.shape[0]
    rg_ref[:, :nodes] = mm_nt(slots_ref[1].T, latent_ref[...]).astype(BF16)
    rg_ref[:, nodes:] = split_rows(wg_ref[...], "hhl").T
    mover.store(rg_ref, rg_out)
    edge_here.wait()
    wo_ref[...] = slots_ref[2].T
    mover.store(wo_ref, wo_out)
    key_here.wait()
    for copy in geo_here:
        copy.wait()
    geo_ref[...] = split_rows(raw_ref[...], "hlh")
    mover.store(geo_ref, geo_out)
    if encoder:
        table_here.wait()
    edge_tiles(0, own_tiles(key_smem, own_pad, shift), FIRST_WINDOW, shift, (key_smem, key_ref, geo_ref), st_ref, rg_ref, wo_ref,
               acc_ref, *stages)
    mover.store(acc_ref, acc_out)
    mover.finish()


def second_kernel(shift, section, own_pad, halo_rows, send_counts, key_smem, *refs):
    refs = list(refs)
    take = lambda n: [refs.pop(0) for _ in range(n)]
    encoder = section == 0
    key_in, square_in, pair_in, st_in, rg_in, acc_in, wo_in, geo_in, latent_in = take(9)
    halos_in = take(len(halo_rows))
    if not encoder:
        (wst_in,) = take(1)
    if send_counts:
        (ids_in,) = take(1)
    (new_out,) = take(1)
    sends_out = take(len(send_counts))
    sems, st_ref, rg_ref, acc_ref, wst_ref, wo_ref, latent_ref, key_ref, geo_ref, slots_ref, halo_ref, new_ref = take(12)
    if send_counts:
        (ids_ref,) = take(1)
        sends_ref = take(len(send_counts))
    stages = refs
    mover = Mover(sems)
    halos_here, at = [], 0
    for ref, rows in zip(halos_in, halo_rows):
        if encoder:
            halos_here.append(mover.start(ref, st_ref.at[:, pl.ds(own_pad + at, rows)]))
        else:
            halos_here.append(mover.start(ref.at[pl.ds(0, rows)], halo_ref.at[pl.ds(at, rows)]))
        at += rows
    if not encoder:
        halos_here.append(mover.start(wst_in, wst_ref))
    tables_here = [
        mover.start(st_in.at[:, pl.ds(0, own_pad)], st_ref.at[:, pl.ds(0, own_pad)]),
        mover.start(rg_in, rg_ref),
        mover.start(wo_in, wo_ref),
        mover.start(key_in, key_ref),
        mover.start(geo_in, geo_ref),
        mover.start(acc_in, acc_ref),
    ]
    late_here = [
        mover.start(latent_in, latent_ref),
        mover.start(pair_in.at[section, 2], slots_ref.at[0]),
        mover.start(pair_in.at[section, 3], slots_ref.at[1]),
        mover.start(square_in.at[3 + 2 * section], slots_ref.at[2]),
    ]
    if send_counts:
        late_here.append(mover.start(ids_in, ids_ref))
    total = at if encoder else halo_ref.shape[0]
    st_ref[:, own_pad + total :] = jnp.zeros((st_ref.shape[0], st_ref.shape[1] - own_pad - total), BF16)
    if not encoder and at < total:
        halo_ref[at:, :] = jnp.zeros((total - at, halo_ref.shape[1]), BF16)
    for copy in halos_here:
        copy.wait()
    if not encoder:
        st_ref[:, own_pad : own_pad + total] = mm_nt(wst_ref[...], halo_ref[...]).astype(BF16)
    for copy in tables_here:
        copy.wait()
    edge_tiles(own_tiles(key_smem, own_pad, shift), key_ref.shape[1] // TILE, SECOND_WINDOW, shift,
               (key_smem, key_ref, geo_ref), st_ref, rg_ref, wo_ref, acc_ref, *stages)
    for copy in late_here:
        copy.wait()
    latent = latent_ref[...]
    pre_act = mm(latent, slots_ref[0]) + mm(acc_ref[...].astype(BF16), slots_ref[1])
    new = (latent.astype(F32) + norm(mm(silu_bf16(pre_act), slots_ref[2]), 1)).astype(BF16)
    new_ref[...] = new
    mover.store(new_ref, new_out)
    if send_counts:
        at = 0
        for send_ref, send_out, count in zip(sends_ref, sends_out, send_counts):
            send_ref[...] = pick_rows(ids_ref, at, count, new)
            mover.store(send_ref, send_out)
            at += up(count, LANES) // LANES
    mover.finish()


SMEM = pl.BlockSpec(memory_space=pltpu.SMEM)
VMEM = pl.BlockSpec(memory_space=pltpu.VMEM)
ANY = pl.BlockSpec(memory_space=pl.ANY)


def call(body, ins, outs, scratch=(), flops=0, first=SMEM, rest=ANY):
    moved = sum(a.size * a.dtype.itemsize for a in outs)
    return pl.pallas_call(
        body,
        in_specs=[first] + [rest] * (len(ins) - 1),
        out_specs=[rest] * len(outs),
        out_shape=outs,
        scratch_shapes=list(scratch),
        compiler_params=pltpu.CompilerParams(vmem_limit_bytes=VMEM_LIMIT),
        cost_estimate=pl.CostEstimate(flops=flops, bytes_accessed=2 * moved, transcendentals=0),
    )(*ins)


def room(*arrays):
    return [pltpu.VMEM(a.shape, a.dtype) for a in arrays]


def room_for(mover_count):
    return [pltpu.SemaphoreType.DMA((mover_count,))]


def shaped(shape, dtype):
    return jax.ShapeDtypeStruct(shape, dtype)


def pair_route(parity, lon_step):
    n_lat, n_lon = lax.axis_size("lat"), lax.axis_size("lon")
    route = []
    for lat in range(n_lat):
        other = lat + 1 if lat % 2 == parity else lat - 1
        if 0 <= other < n_lat:
            route += [(lat * n_lon + (lon - lon_step) % n_lon, other * n_lon + lon) for lon in range(n_lon)]
    return route


def lon_route(parity):
    n_lat, n_lon = lax.axis_size("lat"), lax.axis_size("lon")
    route = []
    for lat in range(n_lat):
        for lon in range(n_lon):
            other = (lon + 1 if lon % 2 == parity else lon - 1) % n_lon
            route.append((lat * n_lon + lon, lat * n_lon + other))
    return route


def order_edges(position, receivers, geometry, shift):
    edges = receivers.shape[0]
    key, *geo = lax.sort(((position << shift) | receivers, *geometry), num_keys=1, is_stable=False)
    return (key,) + tuple(x.reshape(1, edges) for x in (key, *geo))


def per_device(
    grid_feat,
    grid_send,
    g2m_sender,
    g2m_receiver,
    g2m_geom,
    mesh_geom,
    mesh_adjacent_lists,
    mesh_far,
    mesh_sender,
    mesh_receiver,
    mesh_edge_geom,
    embed_in,
    mesh_in,
    geo_in,
    pair_in,
    square_out,
):
    width = embed_in.shape[1]
    own_grid = grid_feat.shape[0]
    slot = grid_send.shape[2]
    nodes = mesh_geom.shape[1]
    near = mesh_adjacent_lists.shape[2]
    far = mesh_far.shape[1] * mesh_far.shape[2]
    edges = mesh_sender.shape[0]
    shift = nodes.bit_length()
    lat_odd = lax.axis_index("lat") % 2
    lon_odd = lax.axis_index("lon") % 2

    tile_shape = (GROUP, width, TILE)
    stages = [pltpu.VMEM(tile_shape, F32)] * 2 + [pltpu.VMEM((GROUP, nodes, TILE), BF16), pltpu.VMEM(tile_shape, F32)]
    weights = [square_out, pair_in]
    acc_shape = shaped((nodes, width), F32)
    latent_shape = shaped((nodes, width), BF16)
    rg_shape = shaped((width, nodes + GEO_ROWS), BF16)
    weight_shape = shaped((width, width), BF16)
    edge_flops = 2 * edges * width * (2 * width + 2 * nodes)

    grid_pad = up(own_grid, LANES)
    grid_t, grid_ids = grid_feat.T, grid_send[0]
    table = shaped((width, grid_pad + FIRST_WINDOW), BF16)
    sent = [shaped((width, slot), BF16)] * 4
    grid_table, *outgoing = call(
        grid_kernel,
        [grid_ids, grid_t, embed_in] + weights,
        [table] + sent,
        room_for(16) + room(grid_ids, grid_t, embed_in, shaped((2, width, width), BF16), table, *sent),
        first=ANY,
    )
    routes = [pair_route(1, 0), pair_route(0, 0), lon_route(1), lon_route(0)]
    arrived = [lax.ppermute(columns, AXES, r) for columns, r in zip(outgoing, routes)]

    offset = g2m_sender - own_grid
    side = offset // slot
    lat_slot = jnp.where((side == 0) == (lat_odd == 0), 1, 0)
    lon_slot = jnp.where((side == 2) == (lon_odd == 0), 3, 2)
    grid_slot = jnp.where(side < 2, lat_slot, lon_slot)
    position = jnp.where(g2m_sender < own_grid, g2m_sender, grid_pad + grid_slot * slot + offset % slot)
    encoder_edges = order_edges(position, g2m_receiver, g2m_geom, shift)

    geo_shape = shaped((GEO_ROWS, edges), BF16)
    raw_shape = shaped((geo_in.shape[1], edges), F32)

    def first_call(section, edge_arrays, own_pad, extra):
        table = shaped((width, own_pad + FIRST_WINDOW), BF16)
        outs = [rg_shape, acc_shape, weight_shape, geo_shape]
        held = [table, rg_shape, acc_shape, weight_shape, weight_shape, latent_shape, edge_arrays[1], raw_shape, geo_shape,
                shaped(geo_in.shape[1:], F32), shaped((3, width, width), BF16)]
        if section == 0:
            outs, held = outs + [latent_shape], held + list(extra[1:])
        else:
            outs = outs + [table, weight_shape]
        return call(
            functools.partial(first_kernel, shift, section, own_pad),
            list(edge_arrays) + [geo_in] + weights + list(extra),
            outs,
            room_for(32) + room(*held) + stages,
            edge_flops,
        )

    rg, acc, wo, geo, latent = first_call(0, encoder_edges, grid_pad, [grid_table, mesh_geom, mesh_in])

    near_lists = mesh_adjacent_lists[0]

    def lat_lists(first):
        left, centre, right = near_lists[first], near_lists[first + 1], near_lists[first + 2]
        return [centre, jnp.where(lon_odd == 1, left, right), jnp.where(lon_odd == 1, right, left)]

    ahead, behind = jnp.concatenate(lat_lists(5)), jnp.concatenate(lat_lists(0))
    sends = [
        jnp.where(lat_odd == 1, ahead, behind),
        jnp.where(lat_odd == 1, behind, ahead),
        jnp.where(lon_odd == 1, near_lists[3], near_lists[4]),
        jnp.where(lon_odd == 1, near_lists[4], near_lists[3]),
        mesh_far[0].reshape(-1),
    ]
    send_counts = tuple(ids.shape[0] for ids in sends)
    send_ids = jnp.concatenate(
        [jnp.pad(ids, (0, up(ids.shape[0], LANES) - ids.shape[0])).reshape(-1, LANES) for ids in sends]
    )
    odd_even, even_odd = pair_route(1, 0), pair_route(0, 0)
    mate, other = lon_route(0), lon_route(1)

    mesh_pad = up(nodes, LANES)
    offset = mesh_sender - nodes
    side = offset // near
    lat_step = jnp.where(side < 3, -1, jnp.where(side < 5, 0, 1))
    lon_step = jnp.where(side < 3, side - 1, jnp.where(side < 5, 2 * side - 7, side - 6))
    by_even = ((lat_step == 1) == (lat_odd == 1)).astype(jnp.int32)
    by_other = ((lon_step == -1) == (lon_odd == 1)).astype(jnp.int32)
    near_slot = jnp.where(
        lat_step == 0, by_other, jnp.where(lon_step == 0, 2 + by_even, 4 + 2 * by_even + by_other)
    )
    halo_row = jnp.where(offset < 8 * near, near_slot * near + offset % near, offset)
    position = jnp.where(mesh_sender < nodes, mesh_sender, mesh_pad + halo_row)
    mesh_edges = order_edges(position, mesh_receiver, mesh_edge_geom, shift)

    sections = geo_in.shape[0]
    halos = arrived
    for section in range(sections):
        encoder, last = section == 0, section == sections - 1
        if encoder:
            own_pad, halo_rows, halo_total = grid_pad, (slot,) * 4, up(4 * slot, LANES)
            smem_key, key = encoder_edges[:2]
            halo_shape = shaped((16, LANES), BF16)
            st = grid_table
        else:
            own_pad, halo_rows, halo_total = mesh_pad, (near,) * 8 + (far,), up(8 * near + far, LANES)
            smem_key, key = mesh_edges[:2]
            halo_shape = shaped((halo_total, width), BF16)
        ins = [smem_key, key] + weights + [st, rg, acc, wo, geo, latent] + list(halos)
        table = shaped((width, own_pad + halo_total + SECOND_WINDOW), BF16)
        held = [table, rg, acc_shape, weight_shape, weight_shape, latent_shape, key, geo_shape, shaped((3, width, width), BF16),
                halo_shape, latent_shape]
        if not encoder:
            ins += [wst]
        counts = () if last else send_counts
        outs = [latent_shape] + [shaped((count, width), BF16) for count in counts]
        if counts:
            ins += [send_ids]
            held += [send_ids] + outs[1:]
        out = call(
            functools.partial(second_kernel, shift, section, own_pad, halo_rows, counts),
            ins,
            outs,
            room_for(36) + room(*held) + stages,
            edge_flops,
        )
        latent = out[0]
        if not last:
            by_odd, by_even, to_mate, to_other, far_out = out[1:]
            by_odd = lax.ppermute(by_odd, AXES, odd_even)
            by_even = lax.ppermute(by_even, AXES, even_odd)
            far_out = far_out.reshape(mesh_far.shape[1], -1, width)
            to_pass = [by_odd[near : 2 * near], by_odd[2 * near :]]
            latent, *to_pass = lax.optimization_barrier((latent, *to_pass))
            far_in = lax.all_to_all(far_out, AXES, split_axis=0, concat_axis=0, tiled=True)
            to_mate, to_other = lax.ppermute(to_mate, AXES, mate), lax.ppermute(to_other, AXES, other)
            passed = [lax.ppermute(to_pass[0], AXES, mate), lax.ppermute(to_pass[1], AXES, other)]
            rg, acc, wo, geo, st, wst = first_call(section + 1, mesh_edges, mesh_pad, [latent])
            by_even, acc, far_in, *passed = lax.optimization_barrier((by_even, acc, far_in, *passed))
            passed += [lax.ppermute(by_even[near : 2 * near], AXES, mate), lax.ppermute(by_even[2 * near :], AXES, other)]
            halos = [to_mate, to_other, by_odd, by_even] + passed
            halos += [far_in.reshape(-1, width)]
    return latent


def solution(mesh):
    in_specs = (
        P(("lat", "lon"), None),
        P(("lat", "lon"), None, None),
        P(("lat", "lon")),
        P(("lat", "lon")),
        P(None, ("lat", "lon")),
        P(None, ("lat", "lon")),
        P(("lat", "lon"), None, None),
        P(("lat", "lon"), None, None),
        P(("lat", "lon")),
        P(("lat", "lon")),
        P(None, ("lat", "lon")),
        P(),
        P(),
        P(),
        P(),
        P(),
    )
    out_specs = P(("lat", "lon"), None)
    return jax.shard_map(
        per_device, mesh=mesh, in_specs=in_specs, out_specs=out_specs, check_vma=False
    )
```

```python
import functools
from typing import NamedTuple

import jax
import jax.numpy as jnp
from jax import lax
from jax.experimental import pallas as pl
from jax.experimental.pallas import tpu as pltpu
from jax.sharding import PartitionSpec as P

EPSILON = 1e-05
TILE = 512
GROUP = 2
FIRST_WINDOW = 256
SECOND_WINDOW = 512
VMEM_LIMIT = 60 * 1024 * 1024
LANES = 128
GEO_ROWS = 16
AXES = ("lat", "lon")
BF16 = jnp.bfloat16
F32 = jnp.float32
NT = (((1,), (1,)), ((), ()))
TN = (((0,), (0,)), ((), ()))


def up(n, m):
    return -(-n // m) * m


def mm(a, b):
    return jnp.dot(a, b, preferred_element_type=F32)


def mm_nt(a, b):
    return lax.dot_general(a, b, NT, preferred_element_type=F32)


def silu_bf16(x):
    half = 0.5 * x
    return (half + half * jnp.tanh(half)).astype(BF16)


def norm(values, axis):
    scale = 1.0 / values.shape[axis]
    centre = values - jnp.sum(values, axis=axis, keepdims=True) * scale
    spread = jnp.sum(centre * centre, axis=axis, keepdims=True) * scale
    return centre * lax.rsqrt(spread + EPSILON)


def one_hot_rows(ids, count):
    rows = lax.broadcasted_iota(jnp.int32, (count, ids.shape[1]), 0)
    return (rows == ids).astype(F32).astype(BF16)


class Place(NamedTuple):
    shift: int
    origin: int
    skip: int
    edges: int

    def sender(self, key):
        return lax.shift_right_logical(key, self.shift) - self.origin

    def lowest(self, ends, tile):
        return self.sender(ends[0][self.skip // TILE + tile])

    def highest(self, ends, tile):
        return self.sender(ends[1][self.skip // TILE + tile])

    def own_tiles(self, ends, own_pad):
        def count(tile, c):
            return c + (self.highest(ends, tile) < own_pad).astype(jnp.int32)

        return lax.fori_loop(0, self.edges // TILE, count, jnp.int32(0))


def split_rows(values, pattern):
    high = values.astype(BF16)
    low = (values - high.astype(F32)).astype(BF16)
    parts = [high if p == "h" else low for p in pattern]
    spare = GEO_ROWS - len(pattern) * values.shape[0]
    parts = [p.astype(F32) for p in parts] + [jnp.zeros((spare, values.shape[1]), F32)]
    return jnp.concatenate(parts, axis=0).astype(BF16)


def edge_tiles(first, last, window, place, edge_refs, st_ref, rg_ref, wo_ref, acc_ref, pre_ref, mid_ref, inc_ref, more_ref):
    ends, key_ref, geo_ref = edge_refs
    node_count = acc_ref.shape[0]

    def tile_lanes(tile):
        return pl.ds(pl.multiple_of(tile * TILE, TILE), TILE)

    def base_of(tile):
        return (place.lowest(ends, tile) // LANES) * LANES

    def windows_of(tile):
        return (place.highest(ends, tile) - base_of(tile)) // window + 1

    def sender_part(tile, start):
        sender = lax.shift_right_logical(key_ref[:, tile_lanes(tile)], place.shift)
        start = pl.multiple_of(start, LANES)
        return mm(st_ref[:, pl.ds(start, window)], one_hot_rows(sender - (start + place.origin), window))

    def load(tile, slot):
        incidence = one_hot_rows(key_ref[:, tile_lanes(tile)] & ((1 << place.shift) - 1), node_count)
        inc_ref[slot] = incidence
        features = jnp.concatenate([incidence, geo_ref[:, tile_lanes(tile)]], axis=0)
        pre_ref[slot] = mm(rg_ref[...], features) + sender_part(tile, base_of(tile)) + more_ref[slot]

    def middle(slot):
        mid_ref[slot] = mm(wo_ref[...], silu_bf16(pre_ref[slot]))

    def store(slot):
        acc_ref[...] += mm_nt(inc_ref[slot], norm(mid_ref[slot], 0).astype(BF16))

    def run(tile, count):
        for slot in range(count):

            @pl.when(windows_of(tile + slot) > 1)
            def _():
                def further(i, c):
                    more_ref[slot] += sender_part(tile + slot, base_of(tile + slot) + i * window)
                    return c

                lax.fori_loop(1, windows_of(tile + slot), further, 0)

        for stage in (lambda s: load(tile + s, s), middle, store):
            for slot in range(count):
                stage(slot)

        for slot in range(count):

            @pl.when(windows_of(tile + slot) > 1)
            def _():
                more_ref[slot] = jnp.zeros(more_ref.shape[1:], F32)

    def together(i, c):
        run(first + i * GROUP, GROUP)
        return c

    def alone(tile, c):
        run(tile, 1)
        return c

    more_ref[...] = jnp.zeros_like(more_ref)
    groups = (last - first) // GROUP
    lax.fori_loop(0, groups, together, 0)
    lax.fori_loop(first + groups * GROUP, last, alone, 0)


def pick_rows(ids_ref, first, count, table):
    rows = []
    for part in range(up(count, LANES) // LANES):
        wide = jnp.broadcast_to(ids_ref[first + part : first + part + 1, :].astype(F32), (LANES, LANES))
        column = wide.T[:, :1].astype(jnp.int32)
        hot = (lax.broadcasted_iota(jnp.int32, (LANES, table.shape[0]), 1) == column).astype(F32).astype(BF16)
        rows.append(mm(hot, table).astype(BF16))
    return jnp.concatenate(rows, axis=0)[:count]


class Mover:
    def __init__(self, sems):
        self.sems, self.used, self.out = sems, 0, []

    def start(self, source, target):
        copy = pltpu.make_async_copy(source, target, self.sems.at[self.used])
        self.used += 1
        copy.start()
        return copy

    def store(self, source, target):
        self.out.append(self.start(source, target))

    def finish(self):
        for copy in self.out:
            copy.wait()


def grid_kernel(ids_in, grid_in, embed_in, square_in, pair_in, st_out, *refs):
    refs = list(refs)
    take = lambda n: [refs.pop(0) for _ in range(n)]
    sends_out = take(4)
    sems, ids_ref, grid_ref, embed_ref, slots_ref, st_ref = take(6)
    sends_ref = refs
    mover = Mover(sems)
    embed_here = mover.start(embed_in, embed_ref)
    grid_here = mover.start(grid_in, grid_ref)
    square_here = mover.start(square_in.at[0], slots_ref.at[0])
    sender_here = mover.start(pair_in.at[0, 0], slots_ref.at[1])
    ids_here = mover.start(ids_in, ids_ref)
    own = grid_ref.shape[1]
    st_ref[:, own:] = jnp.zeros((st_ref.shape[0], st_ref.shape[1] - own), BF16)
    embed_here.wait()
    embed_t = embed_ref[...].T
    grid_here.wait()
    hidden = silu_bf16(mm(embed_t, grid_ref[...]))
    square_here.wait()
    latent = norm(mm(slots_ref[0].T, hidden), 0).astype(BF16)
    sender_here.wait()
    st_ref[:, :own] = mm(slots_ref[1].T, latent).astype(BF16)
    mover.store(st_ref, st_out)
    ids_here.wait()
    lat_odd = lax.axis_index("lat") % 2 == 1
    lon_odd = lax.axis_index("lon") % 2 == 1
    ids = [ids_ref[i : i + 1, :] for i in range(4)]
    asked = [
        jnp.where(lat_odd, ids[1], ids[0]),
        jnp.where(lat_odd, ids[0], ids[1]),
        jnp.where(lon_odd, ids[3], ids[2]),
        jnp.where(lon_odd, ids[2], ids[3]),
    ]
    for wanted, send_ref, send_out in zip(asked, sends_ref, sends_out):
        send_ref[...] = mm(st_ref[:, :own], one_hot_rows(wanted, own)).astype(BF16)
        mover.store(send_ref, send_out)
    mover.finish()


def first_kernel(place, section, own_pad, low_smem, high_smem, *refs):
    refs = list(refs)
    take = lambda n: [refs.pop(0) for _ in range(n)]
    encoder = section == 0
    key_in, *geo_in = take(5)
    wg_in, square_in, pair_in = take(3)
    if encoder:
        st_in, mesh_geom_in, mesh_in = take(3)
    else:
        (latent_in,) = take(1)
    rg_out, acc_out, wo_out, geo_out = take(4)
    if encoder:
        (start_out,) = take(1)
    else:
        st_out, wst_out = take(2)
    sems, st_ref, rg_ref, acc_ref, wst_ref, wo_ref, latent_ref, key_ref, raw_ref, geo_ref, wg_ref, slots_ref = take(12)
    if encoder:
        mesh_geom_ref, mesh_in_ref = take(2)
    stages = refs
    mover = Mover(sems)
    if encoder:
        mesh_geom_here = mover.start(mesh_geom_in, mesh_geom_ref)
        mesh_in_here = mover.start(mesh_in, mesh_in_ref)
        square_mesh_here = mover.start(square_in.at[1], slots_ref.at[0])
    else:
        latent_here = mover.start(latent_in, latent_ref)
        sender_here = mover.start(pair_in.at[section, 0], slots_ref.at[0])
    receiver_here = mover.start(pair_in.at[section, 1], slots_ref.at[1])
    wg_here = mover.start(wg_in.at[section], wg_ref)
    edge_here = mover.start(square_in.at[2 + 2 * section], slots_ref.at[2])
    edge_range = pl.ds(place.skip, place.edges)
    key_here = mover.start(key_in.at[:, edge_range], key_ref)
    geo_here = [mover.start(g.at[:, edge_range], raw_ref.at[pl.ds(i, 1)]) for i, g in enumerate(geo_in)]

    table_here = mover.start(st_in, st_ref) if encoder else None

    acc_ref[...] = jnp.zeros_like(acc_ref)
    if encoder:
        mesh_geom_here.wait()
        mesh_in_here.wait()
        first = lax.dot_general(
            split_rows(mesh_geom_ref[...], "hlh"), split_rows(mesh_in_ref[...], "hhl"), TN, preferred_element_type=F32
        )
        square_mesh_here.wait()
        latent_ref[...] = norm(mm(silu_bf16(first), slots_ref[0]), 1).astype(BF16)
        mover.store(latent_ref, start_out)
    else:
        own = latent_ref.shape[0]
        st_ref[:, own:] = jnp.zeros((st_ref.shape[0], st_ref.shape[1] - own), BF16)
        sender_here.wait()
        wst_ref[...] = slots_ref[0].T
        mover.store(wst_ref, wst_out)
        latent_here.wait()
        st_ref[:, :own] = mm_nt(wst_ref[...], latent_ref[...]).astype(BF16)
        mover.store(st_ref, st_out)
    receiver_here.wait()
    wg_here.wait()
    nodes = latent_ref.shape[0]
    rg_ref[:, :nodes] = mm_nt(slots_ref[1].T, latent_ref[...]).astype(BF16)
    rg_ref[:, nodes:] = split_rows(wg_ref[...], "hhl").T
    mover.store(rg_ref, rg_out)
    edge_here.wait()
    wo_ref[...] = slots_ref[2].T
    mover.store(wo_ref, wo_out)
    key_here.wait()
    for copy in geo_here:
        copy.wait()
    geo_ref[...] = split_rows(raw_ref[...], "hlh")
    mover.store(geo_ref, geo_out)
    if encoder:
        table_here.wait()
    edge_tiles(0, place.own_tiles((low_smem, high_smem), own_pad), FIRST_WINDOW, place, ((low_smem, high_smem), key_ref, geo_ref), st_ref, rg_ref, wo_ref,
               acc_ref, *stages)
    mover.store(acc_ref, acc_out)
    mover.finish()


def second_kernel(place, section, own_pad, halo_rows, send_counts, low_smem, high_smem, *refs):
    refs = list(refs)
    take = lambda n: [refs.pop(0) for _ in range(n)]
    encoder = section == 0
    key_in, square_in, pair_in, st_in, rg_in, acc_in, wo_in, geo_in, latent_in = take(9)
    halos_in = take(len(halo_rows))
    if not encoder:
        (wst_in,) = take(1)
    if send_counts:
        (ids_in,) = take(1)
    (new_out,) = take(1)
    sends_out = take(len(send_counts))
    sems, st_ref, rg_ref, acc_ref, wst_ref, wo_ref, latent_ref, key_ref, geo_ref, slots_ref, halo_ref, new_ref = take(12)
    if send_counts:
        (ids_ref,) = take(1)
        sends_ref = take(len(send_counts))
    stages = refs
    mover = Mover(sems)
    halos_here, at = [], 0
    for ref, rows in zip(halos_in, halo_rows):
        if encoder:
            halos_here.append(mover.start(ref, st_ref.at[:, pl.ds(own_pad + at, rows)]))
        else:
            halos_here.append(mover.start(ref.at[pl.ds(0, rows)], halo_ref.at[pl.ds(at, rows)]))
        at += rows
    if not encoder:
        halos_here.append(mover.start(wst_in, wst_ref))
    tables_here = [
        mover.start(st_in.at[:, pl.ds(0, own_pad)], st_ref.at[:, pl.ds(0, own_pad)]),
        mover.start(rg_in, rg_ref),
        mover.start(wo_in, wo_ref),
        mover.start(key_in.at[:, pl.ds(place.skip, place.edges)], key_ref),
        mover.start(geo_in, geo_ref),
        mover.start(acc_in, acc_ref),
    ]
    late_here = [
        mover.start(latent_in, latent_ref),
        mover.start(pair_in.at[section, 2], slots_ref.at[0]),
        mover.start(pair_in.at[section, 3], slots_ref.at[1]),
        mover.start(square_in.at[3 + 2 * section], slots_ref.at[2]),
    ]
    if send_counts:
        late_here.append(mover.start(ids_in, ids_ref))
    total = at if encoder else halo_ref.shape[0]
    st_ref[:, own_pad + total :] = jnp.zeros((st_ref.shape[0], st_ref.shape[1] - own_pad - total), BF16)
    if not encoder and at < total:
        halo_ref[at:, :] = jnp.zeros((total - at, halo_ref.shape[1]), BF16)
    for copy in halos_here:
        copy.wait()
    if not encoder:
        st_ref[:, own_pad : own_pad + total] = mm_nt(wst_ref[...], halo_ref[...]).astype(BF16)
    for copy in tables_here:
        copy.wait()
    edge_tiles(place.own_tiles((low_smem, high_smem), own_pad), place.edges // TILE, SECOND_WINDOW, place,
               ((low_smem, high_smem), key_ref, geo_ref), st_ref, rg_ref, wo_ref, acc_ref, *stages)
    for copy in late_here:
        copy.wait()
    latent = latent_ref[...]
    pre_act = mm(latent, slots_ref[0]) + mm(acc_ref[...].astype(BF16), slots_ref[1])
    new = (latent.astype(F32) + norm(mm(silu_bf16(pre_act), slots_ref[2]), 1)).astype(BF16)
    new_ref[...] = new
    mover.store(new_ref, new_out)
    if send_counts:
        at = 0
        for send_ref, send_out, count in zip(sends_ref, sends_out, send_counts):
            send_ref[...] = pick_rows(ids_ref, at, count, new)
            mover.store(send_ref, send_out)
            at += up(count, LANES) // LANES
    mover.finish()


SMEM = pl.BlockSpec(memory_space=pltpu.SMEM)
ANY = pl.BlockSpec(memory_space=pl.ANY)


def call(body, ins, outs, scratch=(), flops=0, scalars=2):
    moved = sum(a.size * a.dtype.itemsize for a in outs)
    return pl.pallas_call(
        body,
        in_specs=[SMEM] * scalars + [ANY] * (len(ins) - scalars),
        out_specs=[ANY] * len(outs),
        out_shape=outs,
        scratch_shapes=list(scratch),
        compiler_params=pltpu.CompilerParams(vmem_limit_bytes=VMEM_LIMIT),
        cost_estimate=pl.CostEstimate(flops=flops, bytes_accessed=2 * moved, transcendentals=0),
    )(*ins)


def room(*arrays):
    return [pltpu.VMEM(a.shape, a.dtype) for a in arrays]


def room_for(mover_count):
    return [pltpu.SemaphoreType.DMA((mover_count,))]


def shaped(shape, dtype):
    return jax.ShapeDtypeStruct(shape, dtype)


def pair_route(parity, lon_step):
    n_lat, n_lon = lax.axis_size("lat"), lax.axis_size("lon")
    route = []
    for lat in range(n_lat):
        other = lat + 1 if lat % 2 == parity else lat - 1
        if 0 <= other < n_lat:
            route += [(lat * n_lon + (lon - lon_step) % n_lon, other * n_lon + lon) for lon in range(n_lon)]
    return route


def lon_route(parity):
    n_lat, n_lon = lax.axis_size("lat"), lax.axis_size("lon")
    route = []
    for lat in range(n_lat):
        for lon in range(n_lon):
            other = (lon + 1 if lon % 2 == parity else lon - 1) % n_lon
            route.append((lat * n_lon + lon, lat * n_lon + other))
    return route


def order_edges(sets, shift):
    places, keys, skip, origin = [], [], 0, 0
    for position, receivers, geometry, rows in sets:
        places.append(Place(shift, origin, skip, receivers.shape[0]))
        keys.append(((position + origin) << shift) | receivers)
        skip, origin = skip + receivers.shape[0], origin + rows
    geometry = jnp.concatenate([geometry for _, _, geometry, _ in sets], axis=1)
    key, *geo = lax.sort((jnp.concatenate(keys), *geometry), num_keys=1, is_stable=False)
    return places, (key[::TILE], key[TILE - 1 :: TILE]) + tuple(x.reshape(1, -1) for x in (key, *geo))


def per_device(
    grid_feat,
    grid_send,
    g2m_sender,
    g2m_receiver,
    g2m_geom,
    mesh_geom,
    mesh_adjacent_lists,
    mesh_far,
    mesh_sender,
    mesh_receiver,
    mesh_edge_geom,
    embed_in,
    mesh_in,
    geo_in,
    pair_in,
    square_out,
):
    width = embed_in.shape[1]
    own_grid = grid_feat.shape[0]
    slot = grid_send.shape[2]
    nodes = mesh_geom.shape[1]
    near = mesh_adjacent_lists.shape[2]
    far = mesh_far.shape[1] * mesh_far.shape[2]
    edges = mesh_sender.shape[0]
    shift = nodes.bit_length()
    lat_odd = lax.axis_index("lat") % 2
    lon_odd = lax.axis_index("lon") % 2

    tile_shape = (GROUP, width, TILE)
    stages = [pltpu.VMEM(tile_shape, F32)] * 2 + [pltpu.VMEM((GROUP, nodes, TILE), BF16), pltpu.VMEM(tile_shape, F32)]
    weights = [square_out, pair_in]
    acc_shape = shaped((nodes, width), F32)
    latent_shape = shaped((nodes, width), BF16)
    rg_shape = shaped((width, nodes + GEO_ROWS), BF16)
    weight_shape = shaped((width, width), BF16)
    edge_flops = 2 * edges * width * (2 * width + 2 * nodes)

    grid_pad = up(own_grid, LANES)
    grid_t, grid_ids = grid_feat.T, grid_send[0]
    table = shaped((width, grid_pad + FIRST_WINDOW), BF16)
    sent = [shaped((width, slot), BF16)] * 4
    grid_table, *outgoing = call(
        grid_kernel,
        [grid_ids, grid_t, embed_in] + weights,
        [table] + sent,
        room_for(16) + room(grid_ids, grid_t, embed_in, shaped((2, width, width), BF16), table, *sent),
        scalars=0,
    )
    routes = [pair_route(1, 0), pair_route(0, 0), lon_route(1), lon_route(0)]
    arrived = [lax.ppermute(columns, AXES, r) for columns, r in zip(outgoing, routes)]

    offset = g2m_sender - own_grid
    side = offset // slot
    lat_slot = jnp.where((side == 0) == (lat_odd == 0), 1, 0)
    lon_slot = jnp.where((side == 2) == (lon_odd == 0), 3, 2)
    grid_slot = jnp.where(side < 2, lat_slot, lon_slot)
    position = jnp.where(g2m_sender < own_grid, g2m_sender, grid_pad + grid_slot * slot + offset % slot)
    encoder_set = (position, g2m_receiver, g2m_geom, grid_pad + 4 * slot)

    mesh_pad = up(nodes, LANES)
    offset = mesh_sender - nodes
    side = offset // near
    lat_step = jnp.where(side < 3, -1, jnp.where(side < 5, 0, 1))
    lon_step = jnp.where(side < 3, side - 1, jnp.where(side < 5, 2 * side - 7, side - 6))
    by_even = ((lat_step == 1) == (lat_odd == 1)).astype(jnp.int32)
    by_other = ((lon_step == -1) == (lon_odd == 1)).astype(jnp.int32)
    near_slot = jnp.where(
        lat_step == 0, by_other, jnp.where(lon_step == 0, 2 + by_even, 4 + 2 * by_even + by_other)
    )
    halo_row = jnp.where(offset < 8 * near, near_slot * near + offset % near, offset)
    position = jnp.where(mesh_sender < nodes, mesh_sender, mesh_pad + halo_row)
    mesh_set = (position, mesh_receiver, mesh_edge_geom, mesh_pad + 8 * near + far)
    (encoder_place, mesh_place), edge_arrays = order_edges([encoder_set, mesh_set], shift)

    def first_call(section, place, own_pad, extra):
        geo_shape, raw_shape = shaped((GEO_ROWS, place.edges), BF16), shaped((geo_in.shape[1], place.edges), F32)
        key_shape = shaped((1, place.edges), jnp.int32)
        table = shaped((width, own_pad + FIRST_WINDOW), BF16)
        outs = [rg_shape, acc_shape, weight_shape, geo_shape]
        held = [table, rg_shape, acc_shape, weight_shape, weight_shape, latent_shape, key_shape, raw_shape, geo_shape,
                shaped(geo_in.shape[1:], F32), shaped((3, width, width), BF16)]
        if section == 0:
            outs, held = outs + [latent_shape], held + list(extra[1:])
        else:
            outs = outs + [table, weight_shape]
        return call(
            functools.partial(first_kernel, place, section, own_pad),
            list(edge_arrays) + [geo_in] + weights + list(extra),
            outs,
            room_for(32) + room(*held) + stages,
            edge_flops,
        )

    rg, acc, wo, geo, latent = first_call(0, encoder_place, grid_pad, [grid_table, mesh_geom, mesh_in])

    near_lists = mesh_adjacent_lists[0]

    def lat_lists(first):
        left, centre, right = near_lists[first], near_lists[first + 1], near_lists[first + 2]
        return [centre, jnp.where(lon_odd == 1, left, right), jnp.where(lon_odd == 1, right, left)]

    ahead, behind = jnp.concatenate(lat_lists(5)), jnp.concatenate(lat_lists(0))
    sends = [
        jnp.where(lat_odd == 1, ahead, behind),
        jnp.where(lat_odd == 1, behind, ahead),
        jnp.where(lon_odd == 1, near_lists[3], near_lists[4]),
        jnp.where(lon_odd == 1, near_lists[4], near_lists[3]),
        mesh_far[0].reshape(-1),
    ]
    send_counts = tuple(ids.shape[0] for ids in sends)
    send_ids = jnp.concatenate(
        [jnp.pad(ids, (0, up(ids.shape[0], LANES) - ids.shape[0])).reshape(-1, LANES) for ids in sends]
    )
    odd_even, even_odd = pair_route(1, 0), pair_route(0, 0)
    mate, other = lon_route(0), lon_route(1)


    sections = geo_in.shape[0]
    halos = arrived
    for section in range(sections):
        encoder, last = section == 0, section == sections - 1
        if encoder:
            own_pad, halo_rows, halo_total = grid_pad, (slot,) * 4, up(4 * slot, LANES)
            place = encoder_place
            halo_shape = shaped((16, LANES), BF16)
            st = grid_table
        else:
            own_pad, halo_rows, halo_total = mesh_pad, (near,) * 8 + (far,), up(8 * near + far, LANES)
            place = mesh_place
            halo_shape = shaped((halo_total, width), BF16)
        geo_shape, key_shape = shaped((GEO_ROWS, place.edges), BF16), shaped((1, place.edges), jnp.int32)
        ins = list(edge_arrays[:3]) + weights + [st, rg, acc, wo, geo, latent] + list(halos)
        table = shaped((width, own_pad + halo_total + SECOND_WINDOW), BF16)
        held = [table, rg, acc_shape, weight_shape, weight_shape, latent_shape, key_shape, geo_shape, shaped((3, width, width), BF16),
                halo_shape, latent_shape]
        if not encoder:
            ins += [wst]
        counts = () if last else send_counts
        outs = [latent_shape] + [shaped((count, width), BF16) for count in counts]
        if counts:
            ins += [send_ids]
            held += [send_ids] + outs[1:]
        out = call(
            functools.partial(second_kernel, place, section, own_pad, halo_rows, counts),
            ins,
            outs,
            room_for(36) + room(*held) + stages,
            edge_flops,
        )
        latent = out[0]
        if not last:
            by_odd, by_even, to_mate, to_other, far_out = out[1:]
            by_odd = lax.ppermute(by_odd, AXES, odd_even)
            by_even = lax.ppermute(by_even, AXES, even_odd)
            far_out = far_out.reshape(mesh_far.shape[1], -1, width)
            to_pass = [by_odd[near : 2 * near], by_odd[2 * near :]]
            latent, *to_pass = lax.optimization_barrier((latent, *to_pass))
            far_in = lax.all_to_all(far_out, AXES, split_axis=0, concat_axis=0, tiled=True)
            to_mate, to_other = lax.ppermute(to_mate, AXES, mate), lax.ppermute(to_other, AXES, other)
            passed = [lax.ppermute(to_pass[0], AXES, mate), lax.ppermute(to_pass[1], AXES, other)]
            rg, acc, wo, geo, st, wst = first_call(section + 1, mesh_place, mesh_pad, [latent])
            by_even, acc, far_in, *passed = lax.optimization_barrier((by_even, acc, far_in, *passed))
            passed += [lax.ppermute(by_even[near : 2 * near], AXES, mate), lax.ppermute(by_even[2 * near :], AXES, other)]
            halos = [to_mate, to_other, by_odd, by_even] + passed
            halos += [far_in.reshape(-1, width)]
    return latent


def solution(mesh):
    in_specs = (
        P(("lat", "lon"), None),
        P(("lat", "lon"), None, None),
        P(("lat", "lon")),
        P(("lat", "lon")),
        P(None, ("lat", "lon")),
        P(None, ("lat", "lon")),
        P(("lat", "lon"), None, None),
        P(("lat", "lon"), None, None),
        P(("lat", "lon")),
        P(("lat", "lon")),
        P(None, ("lat", "lon")),
        P(),
        P(),
        P(),
        P(),
        P(),
    )
    out_specs = P(("lat", "lon"), None)
    return jax.shard_map(
        per_device, mesh=mesh, in_specs=in_specs, out_specs=out_specs, check_vma=False
    )
```

```python
import functools
from typing import NamedTuple

import jax
import jax.numpy as jnp
from jax import lax
from jax.experimental import pallas as pl
from jax.experimental.pallas import tpu as pltpu
from jax.sharding import PartitionSpec as P

EPSILON = 1e-05
TILE = 512
GROUP = 2
FIRST_WINDOW = 256
SECOND_WINDOW = 512
VMEM_LIMIT = 60 * 1024 * 1024
LANES = 128
GEO_ROWS = 16
AXES = ("lat", "lon")
BF16 = jnp.bfloat16
F32 = jnp.float32
NT = (((1,), (1,)), ((), ()))
TN = (((0,), (0,)), ((), ()))


def up(n, m):
    return -(-n // m) * m


def mm(a, b):
    return jnp.dot(a, b, preferred_element_type=F32)


def mm_nt(a, b):
    return lax.dot_general(a, b, NT, preferred_element_type=F32)


def silu_bf16(x):
    half = 0.5 * x
    return (half + half * jnp.tanh(half)).astype(BF16)


def norm(values, axis):
    scale = 1.0 / values.shape[axis]
    centre = values - jnp.sum(values, axis=axis, keepdims=True) * scale
    spread = jnp.sum(centre * centre, axis=axis, keepdims=True) * scale
    return centre * lax.rsqrt(spread + EPSILON)


def one_hot_rows(ids, count):
    rows = lax.broadcasted_iota(jnp.int32, (count, ids.shape[1]), 0)
    return (rows == ids).astype(F32).astype(BF16)


class Place(NamedTuple):
    shift: int
    origin: int
    skip: int
    edges: int

    def sender(self, key):
        return lax.shift_right_logical(key, self.shift) - self.origin

    def lowest(self, ends, tile):
        return self.sender(ends[0][self.skip // TILE + tile])

    def highest(self, ends, tile):
        return self.sender(ends[1][self.skip // TILE + tile])

    def own_tiles(self, ends, own_pad):
        def count(tile, c):
            return c + (self.highest(ends, tile) < own_pad).astype(jnp.int32)

        return lax.fori_loop(0, self.edges // TILE, count, jnp.int32(0))


def split_rows(values, pattern):
    high = values.astype(BF16)
    low = (values - high.astype(F32)).astype(BF16)
    parts = [high if p == "h" else low for p in pattern]
    spare = GEO_ROWS - len(pattern) * values.shape[0]
    parts = [p.astype(F32) for p in parts] + [jnp.zeros((spare, values.shape[1]), F32)]
    return jnp.concatenate(parts, axis=0).astype(BF16)


def edge_tiles(first, last, window, place, edge_refs, st_ref, rg_ref, wo_ref, acc_ref, pre_ref, mid_ref, inc_ref, more_ref):
    ends, key_ref, geo_ref = edge_refs
    node_count = acc_ref.shape[0]

    def tile_lanes(tile):
        return pl.ds(pl.multiple_of(tile * TILE, TILE), TILE)

    def base_of(tile):
        return (place.lowest(ends, tile) // LANES) * LANES

    def windows_of(tile):
        return (place.highest(ends, tile) - base_of(tile)) // window + 1

    def sender_part(tile, start):
        sender = lax.shift_right_logical(key_ref[:, tile_lanes(tile)], place.shift)
        start = pl.multiple_of(start, LANES)
        return mm(st_ref[:, pl.ds(start, window)], one_hot_rows(sender - (start + place.origin), window))

    def load(tile, slot):
        incidence = one_hot_rows(key_ref[:, tile_lanes(tile)] & ((1 << place.shift) - 1), node_count)
        inc_ref[slot] = incidence
        features = jnp.concatenate([incidence, geo_ref[:, tile_lanes(tile)]], axis=0)
        pre_ref[slot] = mm(rg_ref[...], features) + sender_part(tile, base_of(tile)) + more_ref[slot]

    def middle(slot):
        mid_ref[slot] = mm(wo_ref[...], silu_bf16(pre_ref[slot]))

    def store(slot):
        acc_ref[...] += mm_nt(inc_ref[slot], norm(mid_ref[slot], 0).astype(BF16))

    def run(tile, count):
        for slot in range(count):

            @pl.when(windows_of(tile + slot) > 1)
            def _():
                def further(i, c):
                    more_ref[slot] += sender_part(tile + slot, base_of(tile + slot) + i * window)
                    return c

                lax.fori_loop(1, windows_of(tile + slot), further, 0)

        for stage in (lambda s: load(tile + s, s), middle, store):
            for slot in range(count):
                stage(slot)

        for slot in range(count):

            @pl.when(windows_of(tile + slot) > 1)
            def _():
                more_ref[slot] = jnp.zeros(more_ref.shape[1:], F32)

    def together(i, c):
        run(first + i * GROUP, GROUP)
        return c

    def alone(tile, c):
        run(tile, 1)
        return c

    more_ref[...] = jnp.zeros_like(more_ref)
    groups = (last - first) // GROUP
    lax.fori_loop(0, groups, together, 0)
    lax.fori_loop(first + groups * GROUP, last, alone, 0)


def pick_rows(ids_ref, first, count, table):
    rows = []
    for part in range(up(count, LANES) // LANES):
        wide = jnp.broadcast_to(ids_ref[first + part : first + part + 1, :].astype(F32), (LANES, LANES))
        column = wide.T[:, :1].astype(jnp.int32)
        hot = (lax.broadcasted_iota(jnp.int32, (LANES, table.shape[0]), 1) == column).astype(F32).astype(BF16)
        rows.append(mm(hot, table).astype(BF16))
    return jnp.concatenate(rows, axis=0)[:count]


class Mover:
    def __init__(self, sems):
        self.sems, self.used, self.out = sems, 0, []

    def start(self, source, target):
        copy = pltpu.make_async_copy(source, target, self.sems.at[self.used])
        self.used += 1
        copy.start()
        return copy

    def store(self, source, target):
        self.out.append(self.start(source, target))

    def finish(self):
        for copy in self.out:
            copy.wait()


def grid_kernel(ids_in, grid_in, embed_in, square_in, pair_in, st_out, *refs):
    refs = list(refs)
    take = lambda n: [refs.pop(0) for _ in range(n)]
    sends_out = take(4)
    sems, ids_ref, grid_ref, embed_ref, slots_ref, st_ref = take(6)
    sends_ref = refs
    mover = Mover(sems)
    embed_here = mover.start(embed_in, embed_ref)
    grid_here = mover.start(grid_in, grid_ref)
    square_here = mover.start(square_in.at[0], slots_ref.at[0])
    sender_here = mover.start(pair_in.at[0, 0], slots_ref.at[1])
    ids_here = mover.start(ids_in, ids_ref)
    own = grid_ref.shape[1]
    st_ref[:, own:] = jnp.zeros((st_ref.shape[0], st_ref.shape[1] - own), BF16)
    embed_here.wait()
    embed_t = embed_ref[...].T
    grid_here.wait()
    hidden = silu_bf16(mm(embed_t, grid_ref[...]))
    square_here.wait()
    latent = norm(mm(slots_ref[0].T, hidden), 0).astype(BF16)
    sender_here.wait()
    st_ref[:, :own] = mm(slots_ref[1].T, latent).astype(BF16)
    mover.store(st_ref, st_out)
    ids_here.wait()
    lat_odd = lax.axis_index("lat") % 2 == 1
    lon_odd = lax.axis_index("lon") % 2 == 1
    ids = [ids_ref[i : i + 1, :] for i in range(4)]
    asked = [
        jnp.where(lat_odd, ids[1], ids[0]),
        jnp.where(lat_odd, ids[0], ids[1]),
        jnp.where(lon_odd, ids[3], ids[2]),
        jnp.where(lon_odd, ids[2], ids[3]),
    ]
    for wanted, send_ref, send_out in zip(asked, sends_ref, sends_out):
        send_ref[...] = mm(st_ref[:, :own], one_hot_rows(wanted, own)).astype(BF16)
        mover.store(send_ref, send_out)
    mover.finish()


def first_kernel(place, section, own_pad, low_smem, high_smem, *refs):
    refs = list(refs)
    take = lambda n: [refs.pop(0) for _ in range(n)]
    encoder = section == 0
    key_in, *geo_in = take(5)
    wg_in, square_in, pair_in = take(3)
    if encoder:
        st_in, mesh_geom_in, mesh_in = take(3)
    else:
        (latent_in,) = take(1)
    rg_out, acc_out, wo_out, geo_out = take(4)
    if encoder:
        (start_out,) = take(1)
    else:
        st_out, wst_out = take(2)
    sems, st_ref, rg_ref, acc_ref, wst_ref, wo_ref, latent_ref, key_ref, raw_ref, geo_ref, wg_ref, slots_ref = take(12)
    if encoder:
        mesh_geom_ref, mesh_in_ref = take(2)
    stages = refs
    mover = Mover(sems)
    if encoder:
        mesh_geom_here = mover.start(mesh_geom_in, mesh_geom_ref)
        mesh_in_here = mover.start(mesh_in, mesh_in_ref)
        square_mesh_here = mover.start(square_in.at[1], slots_ref.at[0])
    else:
        latent_here = mover.start(latent_in, latent_ref)
        sender_here = mover.start(pair_in.at[section, 0], slots_ref.at[0])
    receiver_here = mover.start(pair_in.at[section, 1], slots_ref.at[1])
    wg_here = mover.start(wg_in.at[section], wg_ref)
    edge_here = mover.start(square_in.at[2 + 2 * section], slots_ref.at[2])
    edge_range = pl.ds(place.skip, place.edges)
    key_here = mover.start(key_in.at[:, edge_range], key_ref)
    geo_here = [mover.start(g.at[:, edge_range], raw_ref.at[pl.ds(i, 1)]) for i, g in enumerate(geo_in)]

    table_here = mover.start(st_in, st_ref) if encoder else None

    acc_ref[...] = jnp.zeros_like(acc_ref)
    if encoder:
        mesh_geom_here.wait()
        mesh_in_here.wait()
        first = lax.dot_general(
            split_rows(mesh_geom_ref[...], "hlh"), split_rows(mesh_in_ref[...], "hhl"), TN, preferred_element_type=F32
        )
        square_mesh_here.wait()
        latent_ref[...] = norm(mm(silu_bf16(first), slots_ref[0]), 1).astype(BF16)
        mover.store(latent_ref, start_out)
    else:
        own = latent_ref.shape[0]
        st_ref[:, own:] = jnp.zeros((st_ref.shape[0], st_ref.shape[1] - own), BF16)
        sender_here.wait()
        wst_ref[...] = slots_ref[0].T
        mover.store(wst_ref, wst_out)
        latent_here.wait()
        st_ref[:, :own] = mm_nt(wst_ref[...], latent_ref[...]).astype(BF16)
        mover.store(st_ref, st_out)
    receiver_here.wait()
    wg_here.wait()
    nodes = latent_ref.shape[0]
    rg_ref[:, :nodes] = mm_nt(slots_ref[1].T, latent_ref[...]).astype(BF16)
    rg_ref[:, nodes:] = split_rows(wg_ref[...], "hhl").T
    mover.store(rg_ref, rg_out)
    edge_here.wait()
    wo_ref[...] = slots_ref[2].T
    mover.store(wo_ref, wo_out)
    key_here.wait()
    for copy in geo_here:
        copy.wait()
    geo_ref[...] = split_rows(raw_ref[...], "hlh")
    mover.store(geo_ref, geo_out)
    if encoder:
        table_here.wait()
    edge_tiles(0, place.own_tiles((low_smem, high_smem), own_pad), SECOND_WINDOW if encoder else FIRST_WINDOW, place, ((low_smem, high_smem), key_ref, geo_ref), st_ref, rg_ref, wo_ref,
               acc_ref, *stages)
    mover.store(acc_ref, acc_out)
    mover.finish()


def second_kernel(place, section, own_pad, halo_rows, send_counts, low_smem, high_smem, *refs):
    refs = list(refs)
    take = lambda n: [refs.pop(0) for _ in range(n)]
    encoder = section == 0
    key_in, square_in, pair_in, st_in, rg_in, acc_in, wo_in, geo_in, latent_in = take(9)
    halos_in = take(len(halo_rows))
    if not encoder:
        (wst_in,) = take(1)
    if send_counts:
        (ids_in,) = take(1)
    (new_out,) = take(1)
    sends_out = take(len(send_counts))
    sems, st_ref, rg_ref, acc_ref, wst_ref, wo_ref, latent_ref, key_ref, geo_ref, slots_ref, halo_ref, new_ref = take(12)
    if send_counts:
        (ids_ref,) = take(1)
        sends_ref = take(len(send_counts))
    stages = refs
    mover = Mover(sems)
    halos_here, at = [], 0
    for ref, rows in zip(halos_in, halo_rows):
        if encoder:
            halos_here.append(mover.start(ref, st_ref.at[:, pl.ds(own_pad + at, rows)]))
        else:
            halos_here.append(mover.start(ref.at[pl.ds(0, rows)], halo_ref.at[pl.ds(at, rows)]))
        at += rows
    if not encoder:
        halos_here.append(mover.start(wst_in, wst_ref))
    tables_here = [
        mover.start(st_in.at[:, pl.ds(0, own_pad)], st_ref.at[:, pl.ds(0, own_pad)]),
        mover.start(rg_in, rg_ref),
        mover.start(wo_in, wo_ref),
        mover.start(key_in.at[:, pl.ds(place.skip, place.edges)], key_ref),
        mover.start(geo_in, geo_ref),
        mover.start(acc_in, acc_ref),
    ]
    late_here = [
        mover.start(latent_in, latent_ref),
        mover.start(pair_in.at[section, 2], slots_ref.at[0]),
        mover.start(pair_in.at[section, 3], slots_ref.at[1]),
        mover.start(square_in.at[3 + 2 * section], slots_ref.at[2]),
    ]
    if send_counts:
        late_here.append(mover.start(ids_in, ids_ref))
    total = at if encoder else halo_ref.shape[0]
    st_ref[:, own_pad + total :] = jnp.zeros((st_ref.shape[0], st_ref.shape[1] - own_pad - total), BF16)
    if not encoder and at < total:
        halo_ref[at:, :] = jnp.zeros((total - at, halo_ref.shape[1]), BF16)
    for copy in halos_here:
        copy.wait()
    if not encoder:
        st_ref[:, own_pad : own_pad + total] = mm_nt(wst_ref[...], halo_ref[...]).astype(BF16)
    for copy in tables_here:
        copy.wait()
    edge_tiles(place.own_tiles((low_smem, high_smem), own_pad), place.edges // TILE, SECOND_WINDOW, place,
               ((low_smem, high_smem), key_ref, geo_ref), st_ref, rg_ref, wo_ref, acc_ref, *stages)
    for copy in late_here:
        copy.wait()
    latent = latent_ref[...]
    pre_act = mm(latent, slots_ref[0]) + mm(acc_ref[...].astype(BF16), slots_ref[1])
    new = (latent.astype(F32) + norm(mm(silu_bf16(pre_act), slots_ref[2]), 1)).astype(BF16)
    new_ref[...] = new
    mover.store(new_ref, new_out)
    if send_counts:
        at = 0
        for send_ref, send_out, count in zip(sends_ref, sends_out, send_counts):
            send_ref[...] = pick_rows(ids_ref, at, count, new)
            mover.store(send_ref, send_out)
            at += up(count, LANES) // LANES
    mover.finish()


SMEM = pl.BlockSpec(memory_space=pltpu.SMEM)
ANY = pl.BlockSpec(memory_space=pl.ANY)


def call(body, ins, outs, scratch=(), flops=0, scalars=2):
    moved = sum(a.size * a.dtype.itemsize for a in outs)
    return pl.pallas_call(
        body,
        in_specs=[SMEM] * scalars + [ANY] * (len(ins) - scalars),
        out_specs=[ANY] * len(outs),
        out_shape=outs,
        scratch_shapes=list(scratch),
        compiler_params=pltpu.CompilerParams(vmem_limit_bytes=VMEM_LIMIT),
        cost_estimate=pl.CostEstimate(flops=flops, bytes_accessed=2 * moved, transcendentals=0),
    )(*ins)


def room(*arrays):
    return [pltpu.VMEM(a.shape, a.dtype) for a in arrays]


def room_for(mover_count):
    return [pltpu.SemaphoreType.DMA((mover_count,))]


def shaped(shape, dtype):
    return jax.ShapeDtypeStruct(shape, dtype)


def pair_route(parity, lon_step):
    n_lat, n_lon = lax.axis_size("lat"), lax.axis_size("lon")
    route = []
    for lat in range(n_lat):
        other = lat + 1 if lat % 2 == parity else lat - 1
        if 0 <= other < n_lat:
            route += [(lat * n_lon + (lon - lon_step) % n_lon, other * n_lon + lon) for lon in range(n_lon)]
    return route


def lon_route(parity):
    n_lat, n_lon = lax.axis_size("lat"), lax.axis_size("lon")
    route = []
    for lat in range(n_lat):
        for lon in range(n_lon):
            other = (lon + 1 if lon % 2 == parity else lon - 1) % n_lon
            route.append((lat * n_lon + lon, lat * n_lon + other))
    return route


def order_edges(sets, shift):
    places, keys, skip, origin = [], [], 0, 0
    for position, receivers, geometry, rows in sets:
        places.append(Place(shift, origin, skip, receivers.shape[0]))
        keys.append(((position + origin) << shift) | receivers)
        skip, origin = skip + receivers.shape[0], origin + rows
    geometry = jnp.concatenate([geometry for _, _, geometry, _ in sets], axis=1)
    key, *geo = lax.sort((jnp.concatenate(keys), *geometry), num_keys=1, is_stable=False)
    return places, (key[::TILE], key[TILE - 1 :: TILE]) + tuple(x.reshape(1, -1) for x in (key, *geo))


def per_device(
    grid_feat,
    grid_send,
    g2m_sender,
    g2m_receiver,
    g2m_geom,
    mesh_geom,
    mesh_adjacent_lists,
    mesh_far,
    mesh_sender,
    mesh_receiver,
    mesh_edge_geom,
    embed_in,
    mesh_in,
    geo_in,
    pair_in,
    square_out,
):
    width = embed_in.shape[1]
    own_grid = grid_feat.shape[0]
    slot = grid_send.shape[2]
    nodes = mesh_geom.shape[1]
    near = mesh_adjacent_lists.shape[2]
    far = mesh_far.shape[1] * mesh_far.shape[2]
    edges = mesh_sender.shape[0]
    shift = nodes.bit_length()
    lat_odd = lax.axis_index("lat") % 2
    lon_odd = lax.axis_index("lon") % 2

    tile_shape = (GROUP, width, TILE)
    stages = [pltpu.VMEM(tile_shape, F32)] * 2 + [pltpu.VMEM((GROUP, nodes, TILE), BF16), pltpu.VMEM(tile_shape, F32)]
    weights = [square_out, pair_in]
    acc_shape = shaped((nodes, width), F32)
    latent_shape = shaped((nodes, width), BF16)
    rg_shape = shaped((width, nodes + GEO_ROWS), BF16)
    weight_shape = shaped((width, width), BF16)
    edge_flops = 2 * edges * width * (2 * width + 2 * nodes)

    grid_pad = up(own_grid, LANES)
    grid_t, grid_ids = grid_feat.T, grid_send[0]
    table = shaped((width, grid_pad + SECOND_WINDOW), BF16)
    sent = [shaped((width, slot), BF16)] * 4
    grid_table, *outgoing = call(
        grid_kernel,
        [grid_ids, grid_t, embed_in] + weights,
        [table] + sent,
        room_for(16) + room(grid_ids, grid_t, embed_in, shaped((2, width, width), BF16), table, *sent),
        scalars=0,
    )
    routes = [pair_route(1, 0), pair_route(0, 0), lon_route(1), lon_route(0)]
    arrived = [lax.ppermute(columns, AXES, r) for columns, r in zip(outgoing, routes)]

    offset = g2m_sender - own_grid
    side = offset // slot
    lat_slot = jnp.where((side == 0) == (lat_odd == 0), 1, 0)
    lon_slot = jnp.where((side == 2) == (lon_odd == 0), 3, 2)
    grid_slot = jnp.where(side < 2, lat_slot, lon_slot)
    position = jnp.where(g2m_sender < own_grid, g2m_sender, grid_pad + grid_slot * slot + offset % slot)
    encoder_set = (position, g2m_receiver, g2m_geom, grid_pad + 4 * slot)

    mesh_pad = up(nodes, LANES)
    offset = mesh_sender - nodes
    side = offset // near
    lat_step = jnp.where(side < 3, -1, jnp.where(side < 5, 0, 1))
    lon_step = jnp.where(side < 3, side - 1, jnp.where(side < 5, 2 * side - 7, side - 6))
    by_even = ((lat_step == 1) == (lat_odd == 1)).astype(jnp.int32)
    by_other = ((lon_step == -1) == (lon_odd == 1)).astype(jnp.int32)
    near_slot = jnp.where(
        lat_step == 0, by_other, jnp.where(lon_step == 0, 2 + by_even, 4 + 2 * by_even + by_other)
    )
    halo_row = jnp.where(offset < 8 * near, near_slot * near + offset % near, offset)
    position = jnp.where(mesh_sender < nodes, mesh_sender, mesh_pad + halo_row)
    mesh_set = (position, mesh_receiver, mesh_edge_geom, mesh_pad + 8 * near + far)
    (encoder_place, mesh_place), edge_arrays = order_edges([encoder_set, mesh_set], shift)

    def first_call(section, place, own_pad, extra):
        geo_shape, raw_shape = shaped((GEO_ROWS, place.edges), BF16), shaped((geo_in.shape[1], place.edges), F32)
        key_shape = shaped((1, place.edges), jnp.int32)
        table = shaped((width, own_pad + (SECOND_WINDOW if section == 0 else FIRST_WINDOW)), BF16)
        outs = [rg_shape, acc_shape, weight_shape, geo_shape]
        held = [table, rg_shape, acc_shape, weight_shape, weight_shape, latent_shape, key_shape, raw_shape, geo_shape,
                shaped(geo_in.shape[1:], F32), shaped((3, width, width), BF16)]
        if section == 0:
            outs, held = outs + [latent_shape], held + list(extra[1:])
        else:
            outs = outs + [table, weight_shape]
        return call(
            functools.partial(first_kernel, place, section, own_pad),
            list(edge_arrays) + [geo_in] + weights + list(extra),
            outs,
            room_for(32) + room(*held) + stages,
            edge_flops,
        )

    rg, acc, wo, geo, latent = first_call(0, encoder_place, grid_pad, [grid_table, mesh_geom, mesh_in])

    near_lists = mesh_adjacent_lists[0]

    def lat_lists(first):
        left, centre, right = near_lists[first], near_lists[first + 1], near_lists[first + 2]
        return [centre, jnp.where(lon_odd == 1, left, right), jnp.where(lon_odd == 1, right, left)]

    ahead, behind = jnp.concatenate(lat_lists(5)), jnp.concatenate(lat_lists(0))
    sends = [
        jnp.where(lat_odd == 1, ahead, behind),
        jnp.where(lat_odd == 1, behind, ahead),
        jnp.where(lon_odd == 1, near_lists[3], near_lists[4]),
        jnp.where(lon_odd == 1, near_lists[4], near_lists[3]),
        mesh_far[0].reshape(-1),
    ]
    send_counts = tuple(ids.shape[0] for ids in sends)
    send_ids = jnp.concatenate(
        [jnp.pad(ids, (0, up(ids.shape[0], LANES) - ids.shape[0])).reshape(-1, LANES) for ids in sends]
    )
    odd_even, even_odd = pair_route(1, 0), pair_route(0, 0)
    mate, other = lon_route(0), lon_route(1)


    sections = geo_in.shape[0]
    halos = arrived
    for section in range(sections):
        encoder, last = section == 0, section == sections - 1
        if encoder:
            own_pad, halo_rows, halo_total = grid_pad, (slot,) * 4, up(4 * slot, LANES)
            place = encoder_place
            halo_shape = shaped((16, LANES), BF16)
            st = grid_table
        else:
            own_pad, halo_rows, halo_total = mesh_pad, (near,) * 8 + (far,), up(8 * near + far, LANES)
            place = mesh_place
            halo_shape = shaped((halo_total, width), BF16)
        geo_shape, key_shape = shaped((GEO_ROWS, place.edges), BF16), shaped((1, place.edges), jnp.int32)
        ins = list(edge_arrays[:3]) + weights + [st, rg, acc, wo, geo, latent] + list(halos)
        table = shaped((width, own_pad + halo_total + SECOND_WINDOW), BF16)
        held = [table, rg, acc_shape, weight_shape, weight_shape, latent_shape, key_shape, geo_shape, shaped((3, width, width), BF16),
                halo_shape, latent_shape]
        if not encoder:
            ins += [wst]
        counts = () if last else send_counts
        outs = [latent_shape] + [shaped((count, width), BF16) for count in counts]
        if counts:
            ins += [send_ids]
            held += [send_ids] + outs[1:]
        out = call(
            functools.partial(second_kernel, place, section, own_pad, halo_rows, counts),
            ins,
            outs,
            room_for(36) + room(*held) + stages,
            edge_flops,
        )
        latent = out[0]
        if not last:
            by_odd, by_even, to_mate, to_other, far_out = out[1:]
            by_odd = lax.ppermute(by_odd, AXES, odd_even)
            by_even = lax.ppermute(by_even, AXES, even_odd)
            far_out = far_out.reshape(mesh_far.shape[1], -1, width)
            to_pass = [by_odd[near : 2 * near], by_odd[2 * near :]]
            latent, *to_pass = lax.optimization_barrier((latent, *to_pass))
            far_in = lax.all_to_all(far_out, AXES, split_axis=0, concat_axis=0, tiled=True)
            to_mate, to_other = lax.ppermute(to_mate, AXES, mate), lax.ppermute(to_other, AXES, other)
            passed = [lax.ppermute(to_pass[0], AXES, mate), lax.ppermute(to_pass[1], AXES, other)]
            rg, acc, wo, geo, st, wst = first_call(section + 1, mesh_place, mesh_pad, [latent])
            by_even, acc, far_in, *passed = lax.optimization_barrier((by_even, acc, far_in, *passed))
            passed += [lax.ppermute(by_even[near : 2 * near], AXES, mate), lax.ppermute(by_even[2 * near :], AXES, other)]
            halos = [to_mate, to_other, by_odd, by_even] + passed
            halos += [far_in.reshape(-1, width)]
    return latent


def solution(mesh):
    in_specs = (
        P(("lat", "lon"), None),
        P(("lat", "lon"), None, None),
        P(("lat", "lon")),
        P(("lat", "lon")),
        P(None, ("lat", "lon")),
        P(None, ("lat", "lon")),
        P(("lat", "lon"), None, None),
        P(("lat", "lon"), None, None),
        P(("lat", "lon")),
        P(("lat", "lon")),
        P(None, ("lat", "lon")),
        P(),
        P(),
        P(),
        P(),
        P(),
    )
    out_specs = P(("lat", "lon"), None)
    return jax.shard_map(
        per_device, mesh=mesh, in_specs=in_specs, out_specs=out_specs, check_vma=False
    )
```

```python
import functools
from typing import NamedTuple

import jax
import jax.numpy as jnp
from jax import lax
from jax.experimental import pallas as pl
from jax.experimental.pallas import tpu as pltpu
from jax.sharding import PartitionSpec as P

EPSILON = 1e-05
TILE = 512
GROUP = 2
FIRST_WINDOW = 256
SECOND_WINDOW = 512
VMEM_LIMIT = 60 * 1024 * 1024
LANES = 128
GEO_ROWS = 16
AXES = ("lat", "lon")
BF16 = jnp.bfloat16
F32 = jnp.float32
NT = (((1,), (1,)), ((), ()))
TN = (((0,), (0,)), ((), ()))


def up(n, m):
    return -(-n // m) * m


def mm(a, b):
    return jnp.dot(a, b, preferred_element_type=F32)


def mm_nt(a, b):
    return lax.dot_general(a, b, NT, preferred_element_type=F32)


def silu_bf16(x):
    half = 0.5 * x
    return (half + half * jnp.tanh(half)).astype(BF16)


def norm(values, axis):
    scale = 1.0 / values.shape[axis]
    centre = values - jnp.sum(values, axis=axis, keepdims=True) * scale
    spread = jnp.sum(centre * centre, axis=axis, keepdims=True) * scale
    return centre * lax.rsqrt(spread + EPSILON)


def one_hot_rows(ids, count):
    rows = lax.broadcasted_iota(jnp.int32, (count, ids.shape[1]), 0)
    return (rows == ids).astype(F32).astype(BF16)


class Place(NamedTuple):
    shift: int
    origin: int
    skip: int
    edges: int

    def sender(self, key):
        return lax.shift_right_logical(key, self.shift) - self.origin

    def lowest(self, ends, tile):
        return self.sender(ends[0][self.skip // TILE + tile])

    def highest(self, ends, tile):
        return self.sender(ends[1][self.skip // TILE + tile])

    def own_tiles(self, ends, own_pad):
        def count(tile, c):
            return c + (self.highest(ends, tile) < own_pad).astype(jnp.int32)

        return lax.fori_loop(0, self.edges // TILE, count, jnp.int32(0))


def split_rows(values, pattern):
    high = values.astype(BF16)
    low = (values - high.astype(F32)).astype(BF16)
    parts = [high if p == "h" else low for p in pattern]
    spare = GEO_ROWS - len(pattern) * values.shape[0]
    parts = [p.astype(F32) for p in parts] + [jnp.zeros((spare, values.shape[1]), F32)]
    return jnp.concatenate(parts, axis=0).astype(BF16)


def edge_tiles(first, last, window, place, edge_refs, st_ref, rg_ref, wo_ref, acc_ref, pre_ref, mid_ref, inc_ref, more_ref):
    ends, key_ref, geo_ref = edge_refs
    node_count = acc_ref.shape[0]

    def tile_lanes(tile):
        return pl.ds(pl.multiple_of(tile * TILE, TILE), TILE)

    def base_of(tile):
        return (place.lowest(ends, tile) // LANES) * LANES

    def windows_of(tile):
        return (place.highest(ends, tile) - base_of(tile)) // window + 1

    def sender_part(tile, start):
        sender = lax.shift_right_logical(key_ref[:, tile_lanes(tile)], place.shift)
        start = pl.multiple_of(start, LANES)
        return mm(st_ref[:, pl.ds(start, window)], one_hot_rows(sender - (start + place.origin), window))

    def load(tile, slot):
        incidence = one_hot_rows(key_ref[:, tile_lanes(tile)] & ((1 << place.shift) - 1), node_count)
        inc_ref[slot] = incidence
        features = jnp.concatenate([incidence, geo_ref[:, tile_lanes(tile)]], axis=0)
        pre_ref[slot] = mm(rg_ref[...], features) + sender_part(tile, base_of(tile)) + more_ref[slot]

    def middle(slot):
        mid_ref[slot] = mm(wo_ref[...], silu_bf16(pre_ref[slot]))

    def store(slot):
        acc_ref[...] += mm_nt(inc_ref[slot], norm(mid_ref[slot], 0).astype(BF16))

    def run(tile, count):
        for slot in range(count):

            @pl.when(windows_of(tile + slot) > 1)
            def _():
                def further(i, c):
                    more_ref[slot] += sender_part(tile + slot, base_of(tile + slot) + i * window)
                    return c

                lax.fori_loop(1, windows_of(tile + slot), further, 0)

        for stage in (lambda s: load(tile + s, s), middle, store):
            for slot in range(count):
                stage(slot)

        for slot in range(count):

            @pl.when(windows_of(tile + slot) > 1)
            def _():
                more_ref[slot] = jnp.zeros(more_ref.shape[1:], F32)

    def together(i, c):
        run(first + i * GROUP, GROUP)
        return c

    def alone(tile, c):
        run(tile, 1)
        return c

    more_ref[...] = jnp.zeros_like(more_ref)
    groups = (last - first) // GROUP
    lax.fori_loop(0, groups, together, 0)
    lax.fori_loop(first + groups * GROUP, last, alone, 0)


def pick_rows(ids_ref, first, count, table):
    rows = []
    for part in range(up(count, LANES) // LANES):
        wide = jnp.broadcast_to(ids_ref[first + part : first + part + 1, :].astype(F32), (LANES, LANES))
        column = wide.T[:, :1].astype(jnp.int32)
        hot = (lax.broadcasted_iota(jnp.int32, (LANES, table.shape[0]), 1) == column).astype(F32).astype(BF16)
        rows.append(mm(hot, table).astype(BF16))
    return jnp.concatenate(rows, axis=0)[:count]


class Mover:
    def __init__(self, sems):
        self.sems, self.used, self.out = sems, 0, []

    def start(self, source, target):
        copy = pltpu.make_async_copy(source, target, self.sems.at[self.used])
        self.used += 1
        copy.start()
        return copy

    def store(self, source, target):
        self.out.append(self.start(source, target))

    def finish(self):
        for copy in self.out:
            copy.wait()


def grid_kernel(ids_in, grid_in, embed_in, square_in, pair_in, st_out, *refs):
    refs = list(refs)
    take = lambda n: [refs.pop(0) for _ in range(n)]
    sends_out = take(4)
    sems, ids_ref, grid_ref, embed_ref, slots_ref, st_ref = take(6)
    sends_ref = refs
    mover = Mover(sems)
    embed_here = mover.start(embed_in, embed_ref)
    grid_here = mover.start(grid_in, grid_ref)
    square_here = mover.start(square_in.at[0], slots_ref.at[0])
    sender_here = mover.start(pair_in.at[0, 0], slots_ref.at[1])
    ids_here = mover.start(ids_in, ids_ref)
    own = grid_ref.shape[1]
    st_ref[:, own:] = jnp.zeros((st_ref.shape[0], st_ref.shape[1] - own), BF16)
    embed_here.wait()
    embed_t = embed_ref[...].T
    grid_here.wait()
    hidden = silu_bf16(mm(embed_t, grid_ref[...]))
    square_here.wait()
    latent = norm(mm(slots_ref[0].T, hidden), 0).astype(BF16)
    sender_here.wait()
    st_ref[:, :own] = mm(slots_ref[1].T, latent).astype(BF16)
    mover.store(st_ref, st_out)
    ids_here.wait()
    lat_odd = lax.axis_index("lat") % 2 == 1
    lon_odd = lax.axis_index("lon") % 2 == 1
    ids = [ids_ref[i : i + 1, :] for i in range(4)]
    asked = [
        jnp.where(lat_odd, ids[1], ids[0]),
        jnp.where(lat_odd, ids[0], ids[1]),
        jnp.where(lon_odd, ids[3], ids[2]),
        jnp.where(lon_odd, ids[2], ids[3]),
    ]
    for wanted, send_ref, send_out in zip(asked, sends_ref, sends_out):
        send_ref[...] = mm(st_ref[:, :own], one_hot_rows(wanted, own)).astype(BF16)
        mover.store(send_ref, send_out)
    mover.finish()


def first_kernel(place, section, own_pad, low_smem, high_smem, *refs):
    refs = list(refs)
    take = lambda n: [refs.pop(0) for _ in range(n)]
    encoder = section == 0
    key_in, *geo_in = take(5)
    wg_in, square_in, pair_in = take(3)
    if encoder:
        st_in, mesh_geom_in, mesh_in = take(3)
    else:
        (latent_in,) = take(1)
    rg_out, acc_out, wo_out, geo_out = take(4)
    if encoder:
        (start_out,) = take(1)
    else:
        st_out, wst_out = take(2)
    sems, st_ref, rg_ref, acc_ref, wst_ref, wo_ref, latent_ref, key_ref, raw_ref, geo_ref, wg_ref, slots_ref = take(12)
    if encoder:
        mesh_geom_ref, mesh_in_ref = take(2)
    stages = refs
    mover = Mover(sems)
    if encoder:
        mesh_geom_here = mover.start(mesh_geom_in, mesh_geom_ref)
        mesh_in_here = mover.start(mesh_in, mesh_in_ref)
        square_mesh_here = mover.start(square_in.at[1], slots_ref.at[0])
    else:
        latent_here = mover.start(latent_in, latent_ref)
        sender_here = mover.start(pair_in.at[section, 0], slots_ref.at[0])
    receiver_here = mover.start(pair_in.at[section, 1], slots_ref.at[1])
    wg_here = mover.start(wg_in.at[section], wg_ref)
    edge_here = mover.start(square_in.at[2 + 2 * section], slots_ref.at[2])
    edge_range = pl.ds(place.skip, place.edges)
    key_here = mover.start(key_in.at[:, edge_range], key_ref)
    geo_here = [mover.start(g.at[:, edge_range], raw_ref.at[pl.ds(i, 1)]) for i, g in enumerate(geo_in)]

    table_here = mover.start(st_in, st_ref) if encoder else None

    acc_ref[...] = jnp.zeros_like(acc_ref)
    if encoder:
        mesh_geom_here.wait()
        mesh_in_here.wait()
        first = lax.dot_general(
            split_rows(mesh_geom_ref[...], "hlh"), split_rows(mesh_in_ref[...], "hhl"), TN, preferred_element_type=F32
        )
        square_mesh_here.wait()
        latent_ref[...] = norm(mm(silu_bf16(first), slots_ref[0]), 1).astype(BF16)
        mover.store(latent_ref, start_out)
    else:
        own = latent_ref.shape[0]
        st_ref[:, own:] = jnp.zeros((st_ref.shape[0], st_ref.shape[1] - own), BF16)
        sender_here.wait()
        wst_ref[...] = slots_ref[0].T
        mover.store(wst_ref, wst_out)
        latent_here.wait()
        st_ref[:, :own] = mm_nt(wst_ref[...], latent_ref[...]).astype(BF16)
        mover.store(st_ref, st_out)
    receiver_here.wait()
    wg_here.wait()
    nodes = latent_ref.shape[0]
    rg_ref[:, :nodes] = mm_nt(slots_ref[1].T, latent_ref[...]).astype(BF16)
    rg_ref[:, nodes:] = split_rows(wg_ref[...], "hhl").T
    mover.store(rg_ref, rg_out)
    edge_here.wait()
    wo_ref[...] = slots_ref[2].T
    mover.store(wo_ref, wo_out)
    key_here.wait()
    for copy in geo_here:
        copy.wait()
    geo_ref[...] = split_rows(raw_ref[...], "hlh")
    mover.store(geo_ref, geo_out)
    if encoder:
        table_here.wait()
    edge_tiles(0, place.own_tiles((low_smem, high_smem), own_pad), SECOND_WINDOW if encoder else FIRST_WINDOW, place, ((low_smem, high_smem), key_ref, geo_ref), st_ref, rg_ref, wo_ref,
               acc_ref, *stages)
    mover.store(acc_ref, acc_out)
    mover.finish()


def second_kernel(place, section, own_pad, halo_rows, send_counts, low_smem, high_smem, *refs):
    refs = list(refs)
    take = lambda n: [refs.pop(0) for _ in range(n)]
    encoder = section == 0
    key_in, square_in, pair_in, st_in, rg_in, acc_in, wo_in, geo_in, latent_in = take(9)
    halos_in = take(len(halo_rows))
    if not encoder:
        (wst_in,) = take(1)
    if send_counts:
        (ids_in,) = take(1)
    (new_out,) = take(1)
    sends_out = take(len(send_counts))
    sems, st_ref, rg_ref, acc_ref, wst_ref, wo_ref, latent_ref, key_ref, geo_ref, slots_ref, halo_ref, new_ref = take(12)
    if send_counts:
        (ids_ref,) = take(1)
        sends_ref = take(len(send_counts))
    stages = refs
    mover = Mover(sems)
    halos_here, at = [], 0
    for ref, rows in zip(halos_in, halo_rows):
        if encoder:
            halos_here.append(mover.start(ref, st_ref.at[:, pl.ds(own_pad + at, rows)]))
        else:
            halos_here.append(mover.start(ref.at[pl.ds(0, rows)], halo_ref.at[pl.ds(at, rows)]))
        at += rows
    if not encoder:
        halos_here.append(mover.start(wst_in, wst_ref))
    tables_here = [
        mover.start(st_in.at[:, pl.ds(0, own_pad)], st_ref.at[:, pl.ds(0, own_pad)]),
        mover.start(rg_in, rg_ref),
        mover.start(wo_in, wo_ref),
        mover.start(key_in.at[:, pl.ds(place.skip, place.edges)], key_ref),
        mover.start(geo_in, geo_ref),
        mover.start(acc_in, acc_ref),
    ]
    late_here = [
        mover.start(latent_in, latent_ref),
        mover.start(pair_in.at[section, 2], slots_ref.at[0]),
        mover.start(pair_in.at[section, 3], slots_ref.at[1]),
        mover.start(square_in.at[3 + 2 * section], slots_ref.at[2]),
    ]
    if send_counts:
        late_here.append(mover.start(ids_in, ids_ref))
    total = at if encoder else halo_ref.shape[0]
    st_ref[:, own_pad + total :] = jnp.zeros((st_ref.shape[0], st_ref.shape[1] - own_pad - total), BF16)
    if not encoder and at < total:
        halo_ref[at:, :] = jnp.zeros((total - at, halo_ref.shape[1]), BF16)
    for copy in halos_here:
        copy.wait()
    if not encoder:
        st_ref[:, own_pad : own_pad + total] = mm_nt(wst_ref[...], halo_ref[...]).astype(BF16)
    for copy in tables_here:
        copy.wait()
    edge_tiles(place.own_tiles((low_smem, high_smem), own_pad), place.edges // TILE, SECOND_WINDOW, place,
               ((low_smem, high_smem), key_ref, geo_ref), st_ref, rg_ref, wo_ref, acc_ref, *stages)
    for copy in late_here:
        copy.wait()
    latent = latent_ref[...]
    pre_act = mm(latent, slots_ref[0]) + mm(acc_ref[...].astype(BF16), slots_ref[1])
    new = (latent.astype(F32) + norm(mm(silu_bf16(pre_act), slots_ref[2]), 1)).astype(BF16)
    new_ref[...] = new
    mover.store(new_ref, new_out)
    if send_counts:
        at = 0
        for send_ref, send_out, count in zip(sends_ref, sends_out, send_counts):
            send_ref[...] = pick_rows(ids_ref, at, count, new)
            mover.store(send_ref, send_out)
            at += up(count, LANES) // LANES
    mover.finish()


SMEM = pl.BlockSpec(memory_space=pltpu.SMEM)
ANY = pl.BlockSpec(memory_space=pl.ANY)


def call(body, ins, outs, scratch=(), flops=0, scalars=2):
    moved = sum(a.size * a.dtype.itemsize for a in outs)
    return pl.pallas_call(
        body,
        in_specs=[SMEM] * scalars + [ANY] * (len(ins) - scalars),
        out_specs=[ANY] * len(outs),
        out_shape=outs,
        scratch_shapes=list(scratch),
        compiler_params=pltpu.CompilerParams(vmem_limit_bytes=VMEM_LIMIT),
        cost_estimate=pl.CostEstimate(flops=flops, bytes_accessed=2 * moved, transcendentals=0),
    )(*ins)


def room(*arrays):
    return [pltpu.VMEM(a.shape, a.dtype) for a in arrays]


def room_for(mover_count):
    return [pltpu.SemaphoreType.DMA((mover_count,))]


def shaped(shape, dtype):
    return jax.ShapeDtypeStruct(shape, dtype)


def pair_route(parity, lon_step):
    n_lat, n_lon = lax.axis_size("lat"), lax.axis_size("lon")
    route = []
    for lat in range(n_lat):
        other = lat + 1 if lat % 2 == parity else lat - 1
        if 0 <= other < n_lat:
            route += [(lat * n_lon + (lon - lon_step) % n_lon, other * n_lon + lon) for lon in range(n_lon)]
    return route


def lon_route(parity):
    n_lat, n_lon = lax.axis_size("lat"), lax.axis_size("lon")
    route = []
    for lat in range(n_lat):
        for lon in range(n_lon):
            other = (lon + 1 if lon % 2 == parity else lon - 1) % n_lon
            route.append((lat * n_lon + lon, lat * n_lon + other))
    return route


def order_edges(sets, shift):
    places, keys, skip, origin = [], [], 0, 0
    for position, receivers, geometry, rows in sets:
        places.append(Place(shift, origin, skip, receivers.shape[0]))
        keys.append(((position + origin) << shift) | receivers)
        skip, origin = skip + receivers.shape[0], origin + rows
    geometry = jnp.concatenate([geometry for _, _, geometry, _ in sets], axis=1)
    key, *geo = lax.sort((jnp.concatenate(keys), *geometry), num_keys=1, is_stable=False)
    tiles = key.reshape(-1, TILE)
    return places, (jnp.min(tiles, axis=1), jnp.max(tiles, axis=1)) + tuple(x.reshape(1, -1) for x in (key, *geo))


def per_device(
    grid_feat,
    grid_send,
    g2m_sender,
    g2m_receiver,
    g2m_geom,
    mesh_geom,
    mesh_adjacent_lists,
    mesh_far,
    mesh_sender,
    mesh_receiver,
    mesh_edge_geom,
    embed_in,
    mesh_in,
    geo_in,
    pair_in,
    square_out,
):
    width = embed_in.shape[1]
    own_grid = grid_feat.shape[0]
    slot = grid_send.shape[2]
    nodes = mesh_geom.shape[1]
    near = mesh_adjacent_lists.shape[2]
    far = mesh_far.shape[1] * mesh_far.shape[2]
    edges = mesh_sender.shape[0]
    shift = nodes.bit_length()
    lat_odd = lax.axis_index("lat") % 2
    lon_odd = lax.axis_index("lon") % 2

    tile_shape = (GROUP, width, TILE)
    stages = [pltpu.VMEM(tile_shape, F32)] * 2 + [pltpu.VMEM((GROUP, nodes, TILE), BF16), pltpu.VMEM(tile_shape, F32)]
    weights = [square_out, pair_in]
    acc_shape = shaped((nodes, width), F32)
    latent_shape = shaped((nodes, width), BF16)
    rg_shape = shaped((width, nodes + GEO_ROWS), BF16)
    weight_shape = shaped((width, width), BF16)
    edge_flops = 2 * edges * width * (2 * width + 2 * nodes)

    grid_pad = up(own_grid, LANES)
    grid_t, grid_ids = grid_feat.T, grid_send[0]
    table = shaped((width, grid_pad + SECOND_WINDOW), BF16)
    sent = [shaped((width, slot), BF16)] * 4
    grid_table, *outgoing = call(
        grid_kernel,
        [grid_ids, grid_t, embed_in] + weights,
        [table] + sent,
        room_for(16) + room(grid_ids, grid_t, embed_in, shaped((2, width, width), BF16), table, *sent),
        scalars=0,
    )
    routes = [pair_route(1, 0), pair_route(0, 0), lon_route(1), lon_route(0)]
    arrived = [lax.ppermute(columns, AXES, r) for columns, r in zip(outgoing, routes)]

    offset = g2m_sender - own_grid
    side = offset // slot
    lat_slot = jnp.where((side == 0) == (lat_odd == 0), 1, 0)
    lon_slot = jnp.where((side == 2) == (lon_odd == 0), 3, 2)
    grid_slot = jnp.where(side < 2, lat_slot, lon_slot)
    position = jnp.where(g2m_sender < own_grid, g2m_sender, grid_pad + grid_slot * slot + offset % slot)
    encoder_set = (position, g2m_receiver, g2m_geom, grid_pad + 4 * slot)

    mesh_pad = up(nodes, LANES)
    offset = mesh_sender - nodes
    side = offset // near
    lat_step = jnp.where(side < 3, -1, jnp.where(side < 5, 0, 1))
    lon_step = jnp.where(side < 3, side - 1, jnp.where(side < 5, 2 * side - 7, side - 6))
    by_even = ((lat_step == 1) == (lat_odd == 1)).astype(jnp.int32)
    by_other = ((lon_step == -1) == (lon_odd == 1)).astype(jnp.int32)
    near_slot = jnp.where(
        lat_step == 0, by_other, jnp.where(lon_step == 0, 2 + by_even, 4 + 2 * by_even + by_other)
    )
    halo_row = jnp.where(offset < 8 * near, near_slot * near + offset % near, offset)
    position = jnp.where(mesh_sender < nodes, mesh_sender, mesh_pad + halo_row)
    mesh_set = (position, mesh_receiver, mesh_edge_geom, mesh_pad + 8 * near + far)
    (encoder_place, mesh_place), edge_arrays = order_edges([encoder_set, mesh_set], shift)

    def first_call(section, place, own_pad, extra):
        geo_shape, raw_shape = shaped((GEO_ROWS, place.edges), BF16), shaped((geo_in.shape[1], place.edges), F32)
        key_shape = shaped((1, place.edges), jnp.int32)
        table = shaped((width, own_pad + (SECOND_WINDOW if section == 0 else FIRST_WINDOW)), BF16)
        outs = [rg_shape, acc_shape, weight_shape, geo_shape]
        held = [table, rg_shape, acc_shape, weight_shape, weight_shape, latent_shape, key_shape, raw_shape, geo_shape,
                shaped(geo_in.shape[1:], F32), shaped((3, width, width), BF16)]
        if section == 0:
            outs, held = outs + [latent_shape], held + list(extra[1:])
        else:
            outs = outs + [table, weight_shape]
        return call(
            functools.partial(first_kernel, place, section, own_pad),
            list(edge_arrays) + [geo_in] + weights + list(extra),
            outs,
            room_for(32) + room(*held) + stages,
            edge_flops,
        )

    rg, acc, wo, geo, latent = first_call(0, encoder_place, grid_pad, [grid_table, mesh_geom, mesh_in])

    near_lists = mesh_adjacent_lists[0]

    def lat_lists(first):
        left, centre, right = near_lists[first], near_lists[first + 1], near_lists[first + 2]
        return [centre, jnp.where(lon_odd == 1, left, right), jnp.where(lon_odd == 1, right, left)]

    ahead, behind = jnp.concatenate(lat_lists(5)), jnp.concatenate(lat_lists(0))
    sends = [
        jnp.where(lat_odd == 1, ahead, behind),
        jnp.where(lat_odd == 1, behind, ahead),
        jnp.where(lon_odd == 1, near_lists[3], near_lists[4]),
        jnp.where(lon_odd == 1, near_lists[4], near_lists[3]),
        mesh_far[0].reshape(-1),
    ]
    send_counts = tuple(ids.shape[0] for ids in sends)
    send_ids = jnp.concatenate(
        [jnp.pad(ids, (0, up(ids.shape[0], LANES) - ids.shape[0])).reshape(-1, LANES) for ids in sends]
    )
    odd_even, even_odd = pair_route(1, 0), pair_route(0, 0)
    mate, other = lon_route(0), lon_route(1)


    sections = geo_in.shape[0]
    halos = arrived
    for section in range(sections):
        encoder, last = section == 0, section == sections - 1
        if encoder:
            own_pad, halo_rows, halo_total = grid_pad, (slot,) * 4, up(4 * slot, LANES)
            place = encoder_place
            halo_shape = shaped((16, LANES), BF16)
            st = grid_table
        else:
            own_pad, halo_rows, halo_total = mesh_pad, (near,) * 8 + (far,), up(8 * near + far, LANES)
            place = mesh_place
            halo_shape = shaped((halo_total, width), BF16)
        geo_shape, key_shape = shaped((GEO_ROWS, place.edges), BF16), shaped((1, place.edges), jnp.int32)
        ins = list(edge_arrays[:3]) + weights + [st, rg, acc, wo, geo, latent] + list(halos)
        table = shaped((width, own_pad + halo_total + SECOND_WINDOW), BF16)
        held = [table, rg, acc_shape, weight_shape, weight_shape, latent_shape, key_shape, geo_shape, shaped((3, width, width), BF16),
                halo_shape, latent_shape]
        if not encoder:
            ins += [wst]
        counts = () if last else send_counts
        outs = [latent_shape] + [shaped((count, width), BF16) for count in counts]
        if counts:
            ins += [send_ids]
            held += [send_ids] + outs[1:]
        out = call(
            functools.partial(second_kernel, place, section, own_pad, halo_rows, counts),
            ins,
            outs,
            room_for(36) + room(*held) + stages,
            edge_flops,
        )
        latent = out[0]
        if not last:
            by_odd, by_even, to_mate, to_other, far_out = out[1:]
            by_odd = lax.ppermute(by_odd, AXES, odd_even)
            by_even = lax.ppermute(by_even, AXES, even_odd)
            far_out = far_out.reshape(mesh_far.shape[1], -1, width)
            to_pass = [by_odd[near : 2 * near], by_odd[2 * near :]]
            latent, *to_pass = lax.optimization_barrier((latent, *to_pass))
            far_in = lax.all_to_all(far_out, AXES, split_axis=0, concat_axis=0, tiled=True)
            to_mate, to_other = lax.ppermute(to_mate, AXES, mate), lax.ppermute(to_other, AXES, other)
            passed = [lax.ppermute(to_pass[0], AXES, mate), lax.ppermute(to_pass[1], AXES, other)]
            rg, acc, wo, geo, st, wst = first_call(section + 1, mesh_place, mesh_pad, [latent])
            by_even, acc, far_in, *passed = lax.optimization_barrier((by_even, acc, far_in, *passed))
            passed += [lax.ppermute(by_even[near : 2 * near], AXES, mate), lax.ppermute(by_even[2 * near :], AXES, other)]
            halos = [to_mate, to_other, by_odd, by_even] + passed
            halos += [far_in.reshape(-1, width)]
    return latent


def solution(mesh):
    in_specs = (
        P(("lat", "lon"), None),
        P(("lat", "lon"), None, None),
        P(("lat", "lon")),
        P(("lat", "lon")),
        P(None, ("lat", "lon")),
        P(None, ("lat", "lon")),
        P(("lat", "lon"), None, None),
        P(("lat", "lon"), None, None),
        P(("lat", "lon")),
        P(("lat", "lon")),
        P(None, ("lat", "lon")),
        P(),
        P(),
        P(),
        P(),
        P(),
    )
    out_specs = P(("lat", "lon"), None)
    return jax.shard_map(
        per_device, mesh=mesh, in_specs=in_specs, out_specs=out_specs, check_vma=False
    )
```
